256 devices in a mesh: vocab: 64 (over y, x, z_lo, core), tokens: 4 (over z_hi).
Axes of the slice: x: 4, y: 4, z: 8 (z_hi: 4, z_lo: 2; z = z_hi * 2 + z_lo), core: 2. Of those that a mesh axis runs over, the one named last changes fastest.
Arguments:
- teacher_hidden: bfloat16 [256, 4096], P('vocab', 'tokens'), may hold values from -80 to 80
- student_hidden: bfloat16 [256, 5120], P('vocab', 'tokens'), may hold values from -10 to 10
- teacher_head: bfloat16 [4096, 151936], P('tokens', 'vocab'), may hold values from -1.1 to 1.1
- student_head: bfloat16 [5120, 151936], P('tokens', 'vocab'), may hold values from -6 to 6
- token_ids: int32 [256], P('vocab'), may hold values from 0 to 151935
- valid: int32 [256], P('vocab'), may hold values from 0 to 1, as said below
Outputs:
- loss: float32 [], replicated
- student_grad: bfloat16 [256, 5120], P('vocab', 'tokens')
The draws below stay inside these ranges and needn't reach their ends.
Inputs may be any that keep to these rules, and one draw needn't show every extreme that they name: The last row is always valid.
All inputs are finite; a program needn't handle non-finite values.
Results may differ from the reference program's by a relative error of at most 0.005.
Values may be sent and summed in bfloat16 or wider, within the bound.
No kernel may reach another device: no remote copies, remote signals or barrier semaphores. Data moves between devices by JAX's collectives and lax.ppermute only.
A program may use at most 64 MiB of HBM per device.

```python
import math
import jax
import jax.numpy as jnp
import numpy as np
from jax import lax

V = 151936
DT = 4096
DS = 5120
TOKENS = 256


planted_pairs = 8


def drawn_ids(key):
    first_key = jax.random.fold_in(key, 500)
    second_key = jax.random.fold_in(key, 501)
    first = jax.random.randint(first_key, (planted_pairs,), 0, V)
    second = (first + 1 + jax.random.randint(second_key, (planted_pairs,), 0, V - 1)) % V
    return (first, second)


def planted_vectors(key, salt, width):
    sign_key = jax.random.fold_in(key, salt)
    signs = jax.random.randint(sign_key, (planted_pairs, width), 0, 2).astype(jnp.float32) * 2.0 - 1.0
    halves = jnp.where(jnp.arange(width) < width // 2, 1.0, -1.0).astype(jnp.float32)
    return (signs, signs * halves[None, :])


def rough_rows(key, width, scale):
    entry_key = jax.random.fold_in(key, 24)
    entries = jnp.clip(jax.random.normal(entry_key, (TOKENS, width), jnp.float32), -6.0, 6.0)
    return scale * 3.0 * entries


def hidden_rows(key, salt, width, scale, limit):
    own_key = jax.random.fold_in(key, salt)
    rows = rough_rows(own_key, width, scale)
    return jnp.clip(rows, -limit, limit)


def head_matrix(key, salt, width, scale, limit):
    own_key = jax.random.fold_in(key, salt)
    base = jnp.clip(jax.random.normal(own_key, (width, V), jnp.float32), -6.0, 6.0) * scale
    first_ids, second_ids = drawn_ids(key)
    first, second = planted_vectors(key, salt + 100, width)
    base = base.at[:, first_ids].set(first.T * scale)
    base = base.at[:, second_ids].set(second.T * scale)
    return jnp.clip(base, -limit, limit)


def draw_teacher_hidden(key, part):
    rows = hidden_rows(key, 31, DT, 1.0, 80.0)
    return rows.astype(jnp.bfloat16)


def draw_student_hidden(key, part):
    rows = hidden_rows(key, 37, DS, DS ** (-0.5), 10.0)
    return rows.astype(jnp.bfloat16)


def draw_teacher_head(key, part):
    return head_matrix(key, 31, DT, DT ** (-0.5), 1.1).astype(jnp.bfloat16)


def draw_student_head(key, part):
    return head_matrix(key, 37, DS, 1.0, 6.0).astype(jnp.bfloat16)


def draw_valid(key, part):
    key = jax.random.fold_in(key, 17)
    positions = jnp.arange(TOKENS, dtype=jnp.int32)
    threshold = 250 + 750 * (positions + 1) // TOKENS
    values = jax.random.randint(key, (TOKENS,), 0, 1000)
    return (values < threshold).astype(jnp.int32)


def place_ends(result, stream_key, least, top_value):
    spot = [jax.random.randint(jax.random.fold_in(stream_key, axis), (), 0, length) for axis, length in enumerate(result.shape)]
    longest = result.shape.index(max(result.shape))
    beside = spot[:longest] + [(spot[longest] + 1) % result.shape[longest]] + spot[longest + 1:]
    return result.at[tuple(spot)].set(least).at[tuple(beside)].set(top_value)


def ranked_wide(key, dims, number_of, lean):
    weights = [min(1 << octave, number_of + 1 - (1 << octave)) * (1 << 20) // math.isqrt((1 << octave) ** lean) + 1 for octave in range((number_of + 1).bit_length()) if 1 << octave <= number_of]
    deviation = 1 + sum(weights) // (1 << 30)
    table = np.cumsum(np.array([max(1, weight // deviation) for weight in weights]))
    lot = jax.random.randint(jax.random.fold_in(key, 1), dims, 0, int(table[len(weights) - 1]))
    start = jnp.left_shift(1, jnp.searchsorted(jnp.asarray(table, jnp.int32), lot, side="right").astype(jnp.int32))
    grade = start - 1 + jax.random.randint(jax.random.fold_in(key, 4), dims, 0, 1 << 30) % jnp.minimum(start, number_of + 1 - start)
    return jax.random.permutation(jax.random.fold_in(key, 2), number_of)[grade].astype(jnp.int32)


def setup_inputs(seed: int = 0) -> dict:
    seeds = jax.random.split(jax.random.key(seed), 7)
    teacher_hidden = draw_teacher_hidden(jax.random.fold_in(seeds[6], 71), 0)
    student_hidden = draw_student_hidden(jax.random.fold_in(seeds[6], 71), 0)
    teacher_head = draw_teacher_head(jax.random.fold_in(seeds[6], 71), 0)
    student_head = draw_student_head(jax.random.fold_in(seeds[6], 71), 0)
    token_ids = place_ends(ranked_wide(seeds[4], (TOKENS,), V, 2), jax.random.fold_in(seeds[4], 3), 0, V - 1).astype(jnp.int32)
    valid = draw_valid(jax.random.fold_in(seeds[6], 71), 0)
    return {"teacher_hidden": teacher_hidden, "student_hidden": student_hidden, "teacher_head": teacher_head, "student_head": student_head, "token_ids": token_ids, "valid": valid}


def reference(teacher_hidden, student_hidden, teacher_head, student_head, token_ids, valid):
    teacher_logits = jnp.dot(teacher_hidden, teacher_head, preferred_element_type=jnp.float32)
    student_logits = jnp.dot(student_hidden, student_head, preferred_element_type=jnp.float32)
    teacher_top = jnp.max(teacher_logits, axis=1)
    student_top = jnp.max(student_logits, axis=1)
    teacher_exp = jnp.exp(teacher_logits - teacher_top[:, None])
    teacher_total = jnp.sum(teacher_exp, axis=1)
    student_total = jnp.sum(jnp.exp(student_logits - student_top[:, None]), axis=1)
    cross_term = jnp.sum(teacher_exp * (teacher_logits - student_logits), axis=1)
    teacher_lse = teacher_top + jnp.log(teacher_total)
    student_lse = student_top + jnp.log(student_total)
    columns = jnp.arange(V, dtype=jnp.int32)
    onehot = columns[None, :] == token_ids[:, None]
    picked = jnp.sum(jnp.where(onehot, student_logits, jnp.float32(0.0)), axis=1)
    per_row = cross_term / teacher_total - teacher_lse + 2.0 * student_lse - picked
    mask = valid.astype(jnp.float32)
    loss = jnp.sum(mask * per_row) / jnp.sum(mask)
    teacher_prob = jnp.exp(teacher_logits - teacher_lse[:, None])
    student_prob = jnp.exp(student_logits - student_lse[:, None])
    logit_grad = (mask[:, None] * (2.0 * student_prob - teacher_prob - onehot.astype(jnp.float32))).astype(jnp.bfloat16)
    student_grad = lax.dot_general(logit_grad, student_head, (((1,), (1,)), ((), ())), preferred_element_type=jnp.float32)
    return loss, student_grad.astype(jnp.bfloat16)
```

```python
import functools

import jax
import jax.numpy as jnp
from jax import lax
from jax.experimental import pallas as pl
from jax.experimental.pallas import tpu as pltpu
from jax.sharding import Mesh, PartitionSpec as P

VOCAB = ("y", "x", "zl", "c")
CHIPS = ("y", "x", "zl")
ROWS = 256
LIVE = 192
GROUP = LIVE // 4
LEFT = 1280
BLOCK = 512
STEP = 512.0
BOUND = 63.9
F32 = jnp.float32
BF16 = jnp.bfloat16
I16 = jnp.int16
NT = (((1,), (1,)), ((), ()))
VMEM = pl.BlockSpec(memory_space=pltpu.VMEM)
SMEM = pl.BlockSpec(memory_space=pltpu.SMEM)


def struct(shape, dtype):
    return jax.ShapeDtypeStruct(shape, dtype)


def call(body, outs, *args, scratch=(), mb=32):
    return pl.pallas_call(
        body,
        out_shape=outs,
        in_specs=[SMEM] + [VMEM] * (len(args) - 1),
        out_specs=[VMEM] * len(outs),
        scratch_shapes=scratch,
        compiler_params=pltpu.CompilerParams(vmem_limit_bytes=mb << 20),
    )(*args)


def padded(width):
    return -(-width // 128) * 128


def coded(x):
    return jnp.clip(jnp.round(x * STEP), -32767.0, 32767.0).astype(jnp.int32).astype(I16)


def decoded(x):
    return x.astype(jnp.int32).astype(F32) * (1.0 / STEP)


def iota(shape, axis):
    return lax.broadcasted_iota(jnp.int32, shape, axis)


def order_kernel(scal, own, other, pick_own, pick_other, back_own, back_other, sampled, total):
    me, core = scal[0], scal[1].astype(F32)
    wide = own.shape[0]
    line, lane = iota((wide, wide), 0), iota((wide, wide), 1)
    even = lane - lane % 2
    before = (line < even).astype(F32).astype(BF16)
    same = (line == even).astype(F32).astype(BF16)
    found = []
    for ref in (own, other):
        labels = ref[:, ref.shape[1] - 128 :].astype(F32).T[:8].astype(BF16)
        earlier = jnp.dot(labels, before, preferred_element_type=F32)[3:4]
        here = jnp.dot(labels, same, preferred_element_type=F32)
        ids = here[0:1] + 256.0 * here[1:2] + 65536.0 * here[2:3]
        found.append((here[3:4] > 0.5, earlier, ids, 0.5 * jnp.sum(here[3:4], keepdims=True)))
    start = (core * found[1][3], (1.0 - core) * found[0][3])
    shift = (me * GROUP).astype(F32)
    picked = jnp.zeros((GROUP, 1), F32)
    for (ok, earlier, ids, _), base, pick, back in zip(
        found, start, (pick_own, pick_other), (back_own, back_other)
    ):
        slot = base + earlier
        near = slot - shift
        near = jnp.where(near < 0.0, near + LIVE, near)
        near = jnp.where(ok & (slot < LIVE), near, -1.0)
        column = jnp.broadcast_to(near, (8, wide)).T[:, 0:1]
        row = iota((LIVE, wide), 0).astype(F32)
        odd = iota((LIVE, wide), 1) % 2
        hit = row == near
        slots = iota((wide, LIVE), 1).astype(F32)
        turn = iota((wide, LIVE), 0) % 2
        back_hit = slots == column
        for half in (0, 1):
            pick[half] = (hit & (odd == half)).astype(F32).astype(BF16)
            back[half] = (back_hit & (turn == half)).astype(F32).astype(BF16)
        chosen = (hit & (odd == 0))[:GROUP]
        picked += jnp.sum(jnp.where(chosen, ids, 0.0), axis=1, keepdims=True)
    sampled[...] = jnp.broadcast_to(picked, sampled.shape)
    total[...] = jnp.broadcast_to(found[0][3] + found[1][3], total.shape)


def logits_kernel(
    width, half, scal, pick_own, pick_other, own, other, head,
    up, down, mine, next_left, last_right, peak, rows, logits,
):
    step = pl.program_id(0)

    @pl.when(step == 0)
    def _():
        for k in (0, 1):
            rows[:, k * half : (k + 1) * half] = (
                jnp.dot(pick_own[k], own[:, :half], preferred_element_type=F32)
                + jnp.dot(pick_other[k], other[:, :half], preferred_element_type=F32)
            ).astype(BF16)

    start = pl.multiple_of(step * BLOCK, BLOCK)
    logits[:, pl.ds(start, BLOCK)] = lax.dot_general(
        rows[...], head[...], NT, preferred_element_type=F32
    )

    @pl.when(step == pl.num_programs(0) - 1)
    def _():
        full = padded(width)
        edge = full - 128
        tail = logits[:, edge:full]
        logits[:, edge:full] = jnp.where(iota(tail.shape, 1) < width - edge, tail, 0.0)
        g = GROUP
        up[:, :LEFT] = coded(logits[2 * g : 3 * g, :LEFT])
        up[:, LEFT:] = coded(logits[g : 2 * g, LEFT:full])
        down[:, :LEFT] = coded(logits[3 * g : 4 * g, :LEFT])
        down[:, LEFT:] = coded(logits[2 * g : 3 * g, LEFT:full])
        mine[...] = logits[:g, :full]
        next_left[...] = logits[g : 2 * g, :LEFT]
        last_right[...] = logits[3 * g : 4 * g, LEFT:full]
        peak[...] = jnp.broadcast_to(
            jnp.max(jnp.abs(logits[g:, :full]), keepdims=True), peak.shape
        )


def partial_logits(scal, picks, own, other, head_t, half):
    width, depth = head_t.shape
    full = padded(width)
    outs = (
        struct((GROUP, full), I16),
        struct((GROUP, full), I16),
        struct((GROUP, full), F32),
        struct((GROUP, LEFT), F32),
        struct((GROUP, full - LEFT), F32),
        struct((8, 128), F32),
    )
    steps = pl.cdiv(width, BLOCK)

    def whole(x):
        return pl.BlockSpec(x.shape, lambda i: (0,) * len(x.shape))

    return pl.pallas_call(
        functools.partial(logits_kernel, width, half),
        grid=(steps,),
        out_shape=outs,
        in_specs=[SMEM]
        + [whole(x) for x in (*picks, own, other)]
        + [pl.BlockSpec((BLOCK, depth), lambda i: (i, 0))],
        out_specs=[whole(x) for x in outs],
        scratch_shapes=[
            pltpu.VMEM((LIVE, depth), BF16),
            pltpu.VMEM((LIVE, steps * BLOCK), F32),
        ],
        compiler_params=pltpu.CompilerParams(vmem_limit_bytes=32 << 20),
    )(scal, *picks, own, other, head_t)


def relay_kernel(scal, got_up, got_down, mine, next_left, last_right, up, down, sums, peak):
    left = next_left[...] + decoded(got_up[:, :LEFT])
    right = last_right[...] + decoded(got_down[:, LEFT:])
    up[...] = coded(left)
    down[...] = coded(right)
    sums[:, :LEFT] = mine[:, :LEFT] + decoded(got_down[:, :LEFT])
    sums[:, LEFT:] = mine[:, LEFT:] + decoded(got_up[:, LEFT:])
    top = jnp.maximum(
        jnp.max(jnp.abs(left), keepdims=True), jnp.max(jnp.abs(right), keepdims=True)
    )
    peak[...] = jnp.broadcast_to(top, peak.shape)


def stats_kernel(
    width, scal, t_sum, t_up, t_down, s_sum, s_up, s_down, sampled, p0, p1, p2, p3,
    t_out, s_out, stats, square,
):
    for total, up, down, out in ((t_sum, t_up, t_down, t_out), (s_sum, s_up, s_down, s_out)):
        out[:, :LEFT] = total[:, :LEFT] + decoded(up[...])
        out[:, LEFT:] = total[:, LEFT:] + decoded(down[...])
    t, s = t_out[...], s_out[...]
    column = iota(t.shape, 1)
    inside = column < width
    onehot = (column + scal[2] == sampled[:, 0:1].astype(jnp.int32)) & inside
    t_top = jnp.max(jnp.where(inside, t, -jnp.inf), axis=1, keepdims=True)
    s_top = jnp.max(jnp.where(inside, s, -jnp.inf), axis=1, keepdims=True)
    t_exp = jnp.where(inside, jnp.exp(t - t_top), 0.0)
    s_exp = jnp.where(inside, jnp.exp(s - s_top), 0.0)
    values = (
        t_top,
        s_top,
        jnp.sum(t_exp, axis=1, keepdims=True),
        jnp.sum(s_exp, axis=1, keepdims=True),
        jnp.sum(t_exp * (t - s), axis=1, keepdims=True),
        jnp.sum(jnp.where(onehot, s, 0.0), axis=1, keepdims=True),
    )
    lane = iota((GROUP, 128), 1)
    board = jnp.zeros((GROUP, 128), F32)
    for k, value in enumerate(values):
        board = jnp.where(lane == k, value, board)
    square[...] = jnp.zeros(square.shape, F32)
    square[:GROUP] = board
    flipped = square[...].T[:8]
    peak = jnp.maximum(jnp.maximum(p0[...], p1[...]), jnp.maximum(p2[...], p3[...]))
    stats[...] = jnp.where(iota((8, 128), 0) == 6, peak, flipped)


def grad_kernel(width, scal, every, t_ref, s_ref, sampled, total, left, right, tally):
    e = every[...]
    most = jnp.max(e, axis=0)
    t_top, s_top, peak = most[0:1], most[1:2], most[6:7]
    t_scale = jnp.exp(e[:, 0:1] - t_top[None])
    s_scale = jnp.exp(e[:, 1:2] - s_top[None])
    t_total = jnp.sum(e[:, 2:3] * t_scale, axis=0)
    s_total = jnp.sum(e[:, 3:4] * s_scale, axis=0)
    cross = jnp.sum(e[:, 4:5] * t_scale, axis=0)
    picked = jnp.sum(e[:, 5:6], axis=0)
    t_lse = t_top + jnp.log(t_total)
    s_lse = s_top + jnp.log(s_total)
    per_row = cross / t_total - t_lse + 2.0 * s_lse - picked
    first = scal[0] * GROUP
    count = total[0:1, 0:1].astype(jnp.int32)
    lane = iota((1, 128), 1)
    live = (lane < GROUP) & (lane + first < count)
    part = jnp.sum(jnp.where(live, per_row, 0.0), axis=1, keepdims=True)
    spot = iota((8, 128), 1)
    tally[...] = jnp.where(spot == 0, part, jnp.where(spot == 1, jnp.max(peak, keepdims=True), 0.0))
    line = iota((8, 128), 0)
    turned = jnp.where(line == 0, t_lse, s_lse).T
    t_col, s_col = turned[:GROUP, 0:1], turned[:GROUP, 1:2]
    t, s = t_ref[...], s_ref[...]
    column = iota(t.shape, 1)
    onehot = (column + scal[2] == sampled[:, 0:1].astype(jnp.int32)).astype(F32)
    grad = 2.0 * jnp.exp(s - s_col) - jnp.exp(t - t_col) - onehot
    keep = (column < width) & (iota(t.shape, 0) + first < count)
    grad = jnp.where(keep, grad, 0.0)
    left[...] = grad[:, :LEFT].astype(BF16)
    right[...] = grad[:, LEFT:].astype(BF16)


def back_kernel(
    width, half, a0, b0, a1, b1, a2, b2, a3, b3, back_own, back_other, head,
    mine, theirs, grads, total,
):
    step = pl.program_id(0)
    full = padded(width)

    @pl.when(step == 0)
    def _():
        for k, (a, b) in enumerate(((a0, b0), (a1, b1), (a2, b2), (a3, b3))):
            grads[k * GROUP : (k + 1) * GROUP, :LEFT] = a[...]
            grads[k * GROUP : (k + 1) * GROUP, LEFT:full] = b[...]
        grads[:, full:] = jnp.zeros((LIVE, grads.shape[1] - full), BF16)
        total[...] = jnp.zeros(total.shape, F32)

    start = pl.multiple_of(step * BLOCK, BLOCK)
    block = head[...]
    block = jnp.where(iota(block.shape, 0) + start < width, block, jnp.zeros_like(block))
    total[...] += jnp.dot(grads[:, pl.ds(start, BLOCK)], block, preferred_element_type=F32)

    @pl.when(step == pl.num_programs(0) - 1)
    def _():
        x = total[...]
        high = x.astype(BF16)
        low = (x - high.astype(F32)).astype(BF16)
        for back, out in ((back_own, mine), (back_other, theirs)):
            y = jnp.zeros(out.shape, F32)
            for k in (0, 1):
                cut = slice(k * half, (k + 1) * half)
                y += jnp.dot(back[k], high[:, cut], preferred_element_type=F32)
                y += jnp.dot(back[k], low[:, cut], preferred_element_type=F32)
            out[...] = y


def hidden_grad(pieces, backs, head_t):
    width, depth = head_t.shape
    steps = pl.cdiv(width, BLOCK)
    outs = (struct((ROWS, depth // 2), F32),) * 2

    def whole(x):
        return pl.BlockSpec(x.shape, lambda i: (0,) * len(x.shape))

    return pl.pallas_call(
        functools.partial(back_kernel, width, depth // 2),
        grid=(steps,),
        out_shape=outs,
        in_specs=[whole(x) for x in (*pieces, *backs)]
        + [pl.BlockSpec((BLOCK, depth), lambda i: (i, 0))],
        out_specs=[whole(x) for x in outs],
        scratch_shapes=[
            pltpu.VMEM((LIVE, steps * BLOCK), BF16),
            pltpu.VMEM((LIVE, depth), F32),
        ],
        compiler_params=pltpu.CompilerParams(vmem_limit_bytes=32 << 20),
    )(*pieces, *backs, head_t)


def hop(x, by):
    return lax.ppermute(x, "t", [(i, (i + by) % 4) for i in range(4)])


def swap_cores(x):
    return lax.ppermute(x, "c", [(0, 1), (1, 0)])


def spread(x, axes, n):
    return lax.all_to_all(
        jnp.broadcast_to(x[None], (n,) + x.shape), axes, split_axis=0, concat_axis=0, tiled=True
    )


def pack_labels(token_ids, valid):
    parts = (token_ids % 256, (token_ids // 256) % 256, token_ids // 65536, valid)
    rows = jnp.stack(parts, axis=1).astype(BF16)
    return jnp.pad(rows[:, None], ((0, 0), (0, 1), (0, 124))).reshape(8, 128)


def short_way(teacher_hidden, student_hidden, teacher_head, student_head, token_ids, valid):
    dt, ds = teacher_hidden.shape[1], student_hidden.shape[1]
    width = teacher_head.shape[1]
    full = padded(width)
    scal = jnp.stack(
        [lax.axis_index("t"), lax.axis_index("c"), lax.axis_index(VOCAB) * width]
    ).astype(jnp.int32)
    first = jnp.concatenate(
        [teacher_hidden.reshape(8, dt // 2), pack_labels(token_ids, valid)], axis=1
    )
    t_own = spread(first, CHIPS, 32).reshape(ROWS, dt // 2 + 128)
    t_other = swap_cores(t_own)
    s_own = spread(student_hidden.reshape(8, ds // 2), CHIPS, 32).reshape(ROWS, ds // 2)
    s_other = swap_cores(s_own)
    pick_own, pick_other, back_own, back_other, sampled, total = call(
        order_kernel,
        (struct((2, LIVE, ROWS), BF16),) * 2
        + (struct((2, ROWS, LIVE), BF16),) * 2
        + (struct((GROUP, 128), F32), struct((8, 128), F32)),
        scal, t_own, t_other,
    )
    sums, peaks = [], []
    for own, other, head, depth in (
        (t_own, t_other, teacher_head, dt),
        (s_own, s_other, student_head, ds),
    ):
        up, down, mine, next_left, last_right, peak = partial_logits(
            scal, (pick_own, pick_other), own, other, head.T, depth // 2
        )
        got_up, got_down = hop(up, 1), hop(down, -1)
        up, down, mine, late = call(
            relay_kernel,
            (
                struct((GROUP, LEFT), I16),
                struct((GROUP, full - LEFT), I16),
                struct((GROUP, full), F32),
                struct((8, 128), F32),
            ),
            scal, got_up, got_down, mine, next_left, last_right,
        )
        sums += [mine, hop(up, 1), hop(down, -1)]
        peaks += [peak, late]
    t_logits, s_logits, stats = call(
        functools.partial(stats_kernel, width),
        (struct((GROUP, full), F32),) * 2 + (struct((8, 128), F32),),
        scal, *sums, sampled, *peaks,
        scratch=[pltpu.VMEM((128, 128), F32)],
    )
    every = spread(stats, VOCAB, 64)
    a0, b0, tally = call(
        functools.partial(grad_kernel, width),
        (
            struct((GROUP, LEFT), BF16),
            struct((GROUP, full - LEFT), BF16),
            struct((8, 128), F32),
        ),
        scal, every, t_logits, s_logits, sampled, total,
    )
    a3, b1 = hop(a0, 1), hop(b0, -1)
    b3, a1 = hop(b0, 1), hop(a0, -1)
    a2, b2 = hop(a3, 1), hop(b1, -1)
    tallies = (tally, hop(tally, 2), hop(tally, 1), hop(tally, -1))
    mine, theirs = hidden_grad((a0, b0, a1, b1, a2, b2, a3, b3), (back_own, back_other), student_head.T)
    pair = (mine + swap_cores(theirs)).astype(BF16).reshape(32, 8, ds // 2)
    got = lax.all_to_all(pair, CHIPS, split_axis=0, concat_axis=0, tiled=True)
    grad = jnp.sum(got.astype(F32), axis=0).astype(BF16).reshape(4, ds)
    count = total[0, 0]
    part = (tallies[0][0, 0] + tallies[1][0, 0]) + (tallies[2][0, 0] + tallies[3][0, 0])
    peak = jnp.maximum(
        jnp.maximum(tallies[0][0, 1], tallies[1][0, 1]),
        jnp.maximum(tallies[2][0, 1], tallies[3][0, 1]),
    )
    return part / count, grad, (count <= LIVE) & (peak < BOUND)


def long_way(teacher_hidden, student_hidden, teacher_head, student_head, token_ids, valid):
    ds = student_hidden.shape[1]
    width = teacher_head.shape[1]
    group = ROWS // 4
    labels = jnp.pad(jnp.stack([token_ids, valid]), ((0, 6), (0, 124)))
    labels = spread(labels, VOCAB, 64)[:, :2, :4].transpose(1, 0, 2).reshape(2, ROWS)

    def logits(hidden, head):
        rows = spread(hidden, VOCAB, 64).reshape(ROWS, hidden.shape[1])
        part = jnp.dot(rows, head, preferred_element_type=F32).reshape(4, group, width)
        return jnp.sum(lax.all_to_all(part, "t", split_axis=0, concat_axis=0, tiled=True), axis=0)

    teacher_logits = logits(teacher_hidden, teacher_head)
    student_logits = logits(student_hidden, student_head)
    here = lax.dynamic_slice_in_dim(labels, lax.axis_index("t") * group, group, 1)
    sampled, mask = here[0], here[1].astype(F32)
    columns = lax.axis_index(VOCAB) * width + jnp.arange(width, dtype=jnp.int32)
    onehot = columns[None, :] == sampled[:, None]
    t_top = jnp.max(teacher_logits, axis=1)
    s_top = jnp.max(student_logits, axis=1)
    t_exp = jnp.exp(teacher_logits - t_top[:, None])
    s_exp = jnp.exp(student_logits - s_top[:, None])
    stats = jnp.stack(
        [
            t_top,
            s_top,
            jnp.sum(t_exp, axis=1),
            jnp.sum(s_exp, axis=1),
            jnp.sum(t_exp * (teacher_logits - student_logits), axis=1),
            jnp.sum(jnp.where(onehot, student_logits, F32(0.0)), axis=1),
        ]
    )
    every = spread(jnp.pad(stats, ((0, 2), (0, 128 - group))), VOCAB, 64)[:, :, :group]
    teacher_top = jnp.max(every[:, 0], axis=0)
    student_top = jnp.max(every[:, 1], axis=0)
    t_scale = jnp.exp(every[:, 0] - teacher_top)
    s_scale = jnp.exp(every[:, 1] - student_top)
    teacher_total = jnp.sum(every[:, 2] * t_scale, axis=0)
    student_total = jnp.sum(every[:, 3] * s_scale, axis=0)
    cross_term = jnp.sum(every[:, 4] * t_scale, axis=0)
    picked = jnp.sum(every[:, 5], axis=0)
    teacher_lse = teacher_top + jnp.log(teacher_total)
    student_lse = student_top + jnp.log(student_total)
    per_row = cross_term / teacher_total - teacher_lse + 2.0 * student_lse - picked
    loss = lax.psum(jnp.sum(mask * per_row), "t") / jnp.sum(labels[1]).astype(F32)
    teacher_prob = jnp.exp(teacher_logits - teacher_lse[:, None])
    student_prob = jnp.exp(student_logits - student_lse[:, None])
    logit_grad = (
        mask[:, None] * (2.0 * student_prob - teacher_prob - onehot.astype(F32))
    ).astype(BF16)
    part = lax.dot_general(
        lax.all_gather(logit_grad, "t", axis=0, tiled=True), student_head, NT,
        preferred_element_type=F32,
    )
    got = lax.all_to_all(part.reshape(64, 4, ds), VOCAB, split_axis=0, concat_axis=0, tiled=True)
    return loss, jnp.sum(got, axis=0).astype(BF16)


def on_device(*args):
    loss, grad, fits = short_way(*args)
    return lax.cond(fits, lambda *_: (loss, grad), long_way, *args)


def solution(mesh):
    fine = Mesh(mesh.devices.reshape(4, 4, 2, 2, 4), VOCAB + ("t",))
    in_specs = (
        P(VOCAB, "t"),
        P(VOCAB, "t"),
        P("t", VOCAB),
        P("t", VOCAB),
        P(VOCAB),
        P(VOCAB),
    )
    return jax.shard_map(
        on_device, mesh=fine, in_specs=in_specs, out_specs=(P(), P(VOCAB, "t")), check_vma=False
    )
```

```python
import functools

import jax
import jax.numpy as jnp
from jax import lax
from jax.experimental import pallas as pl
from jax.experimental.pallas import tpu as pltpu
from jax.sharding import Mesh, PartitionSpec as P

VOCAB = ("y", "x", "zl", "c")
CHIPS = ("y", "x", "zl")
ROWS = 256
LIVE = 192
GROUP = LIVE // 4
LEFT = 1280
BLOCK = 512
STEP = 1024.0
BOUND = 31.9
F32 = jnp.float32
BF16 = jnp.bfloat16
I16 = jnp.int16
NT = (((1,), (1,)), ((), ()))
VMEM = pl.BlockSpec(memory_space=pltpu.VMEM)
SMEM = pl.BlockSpec(memory_space=pltpu.SMEM)


def struct(shape, dtype):
    return jax.ShapeDtypeStruct(shape, dtype)


def call(body, outs, *args, scratch=(), scalars=0):
    return pl.pallas_call(
        body,
        out_shape=outs,
        in_specs=[SMEM] + [VMEM] * (len(args) - 1),
        out_specs=[VMEM] * (len(outs) - scalars) + [SMEM] * scalars,
        scratch_shapes=scratch,
        compiler_params=pltpu.CompilerParams(vmem_limit_bytes=32 << 20),
    )(*args)


def padded(width):
    return -(-width // 128) * 128


def coded(x):
    return jnp.clip(jnp.round(x * STEP), -32767.0, 32767.0).astype(jnp.int32).astype(I16)


def decoded(x):
    return x.astype(jnp.int32).astype(F32) * (1.0 / STEP)


def iota(shape, axis):
    return lax.broadcasted_iota(jnp.int32, shape, axis)


def order_kernel(at, scal, own, other, pick_own, pick_other, back_own, back_other, sampled, total):
    me, core = scal[0], scal[1].astype(F32)
    wide = own.shape[0]
    line, lane = iota((wide, wide), 0), iota((wide, wide), 1)
    even = lane - lane % 2
    before = (line < even).astype(F32).astype(BF16)
    same = (line == even).astype(F32).astype(BF16)
    found = []
    for ref in (own, other):
        labels = ref[:, at : at + 128].astype(F32).T[:8].astype(BF16)
        earlier = jnp.dot(labels, before, preferred_element_type=F32)[3:4]
        here = jnp.dot(labels, same, preferred_element_type=F32)
        ids = here[0:1] + 256.0 * here[1:2] + 65536.0 * here[2:3]
        found.append((here[3:4] > 0.5, earlier, ids, 0.5 * jnp.sum(here[3:4], keepdims=True)))
    start = (core * found[1][3], (1.0 - core) * found[0][3])
    shift = (me * GROUP).astype(F32)
    picked = jnp.zeros((GROUP, 1), F32)
    for (ok, earlier, ids, _), base, pick, back in zip(
        found, start, (pick_own, pick_other), (back_own, back_other)
    ):
        slot = base + earlier
        near = slot - shift
        near = jnp.where(near < 0.0, near + LIVE, near)
        near = jnp.where(ok & (slot < LIVE), near, -1.0)
        column = jnp.broadcast_to(near, (8, wide)).T[:, 0:1]
        row = iota((LIVE, wide), 0).astype(F32)
        odd = iota((LIVE, wide), 1) % 2
        hit = row == near
        slots = iota((wide, LIVE), 1).astype(F32)
        turn = iota((wide, LIVE), 0) % 2
        back_hit = slots == column
        for half in (0, 1):
            pick[half] = (hit & (odd == half)).astype(F32).astype(BF16)
            back[half] = (back_hit & (turn == half)).astype(F32).astype(BF16)
        chosen = (hit & (odd == 0))[:GROUP]
        picked += jnp.sum(jnp.where(chosen, ids, 0.0), axis=1, keepdims=True)
    sampled[...] = jnp.broadcast_to(picked, sampled.shape)
    total[...] = jnp.broadcast_to(found[0][3] + found[1][3], total.shape)


def logits_kernel(
    width, half, at, far, near, relayed, scal, pick_own, pick_other, own, other, head,
    first, direct, mine, held, peak, rows, logits,
):
    for k in (0, 1):
        rows[:, k * half : (k + 1) * half] = (
            jnp.dot(pick_own[k], own[:, at : at + half], preferred_element_type=F32)
            + jnp.dot(pick_other[k], other[:, at : at + half], preferred_element_type=F32)
        ).astype(BF16)
    full = padded(width)
    edge = full - 128
    logits[:, edge:full] = jnp.zeros((LIVE, 128), F32)
    for start in range(0, width, BLOCK):
        stop = min(start + BLOCK, width)
        logits[:, start:stop] = lax.dot_general(
            rows[...], head[start:stop], NT, preferred_element_type=F32
        )
    g = GROUP
    first[...] = coded(logits[far * g : (far + 1) * g])
    direct[...] = coded(logits[near * g : (near + 1) * g])
    mine[...] = logits[:g]
    held[...] = logits[relayed * g : (relayed + 1) * g]
    peak[...] = jnp.broadcast_to(jnp.max(jnp.abs(logits[g:]), keepdims=True), peak.shape)


def partial_logits(scal, picks, own, other, head_t, at, near, relayed):
    width, depth = head_t.shape
    full = padded(width)
    outs = (
        struct((GROUP, full), I16),
        struct((GROUP, full), I16),
        struct((GROUP, full), F32),
        struct((GROUP, full), F32),
        struct((8, 128), F32),
    )
    return call(
        functools.partial(logits_kernel, width, depth // 2, at, 2, near, relayed),
        outs, scal, *picks, own, other, head_t,
        scratch=[pltpu.VMEM((LIVE, depth), BF16), pltpu.VMEM((LIVE, full), F32)],
    )


def relay_kernel(scal, got, held, out, peak):
    total = held[...] + decoded(got[...])
    out[...] = coded(total)
    peak[...] = jnp.broadcast_to(jnp.max(jnp.abs(total), keepdims=True), peak.shape)


def stats_kernel(
    width, scal, t_mine, t_direct, t_late, s_mine, s_direct, s_late, sampled, p0, p1, p2, p3,
    t_out, s_out, stats, square,
):
    t = t_mine[...] + decoded(t_direct[...]) + decoded(t_late[...])
    s = s_mine[...] + decoded(s_direct[...]) + decoded(s_late[...])
    t_out[...] = t
    s_out[...] = s
    column = iota(t.shape, 1)
    inside = column < width
    onehot = (column + scal[2] == sampled[:, 0:1].astype(jnp.int32)) & inside
    t_top = jnp.max(jnp.where(inside, t, -jnp.inf), axis=1, keepdims=True)
    s_top = jnp.max(jnp.where(inside, s, -jnp.inf), axis=1, keepdims=True)
    t_exp = jnp.where(inside, jnp.exp(t - t_top), 0.0)
    s_exp = jnp.where(inside, jnp.exp(s - s_top), 0.0)
    values = (
        t_top,
        s_top,
        jnp.sum(t_exp, axis=1, keepdims=True),
        jnp.sum(s_exp, axis=1, keepdims=True),
        jnp.sum(t_exp * (t - s), axis=1, keepdims=True),
        jnp.sum(jnp.where(onehot, s, 0.0), axis=1, keepdims=True),
    )
    lane = iota((GROUP, 128), 1)
    board = jnp.zeros((GROUP, 128), F32)
    for k, value in enumerate(values):
        board = jnp.where(lane == k, value, board)
    square[...] = jnp.zeros(square.shape, F32)
    square[:GROUP] = board
    flipped = square[...].T[:8]
    peak = jnp.maximum(jnp.maximum(p0[...], p1[...]), jnp.maximum(p2[...], p3[...]))
    stats[...] = jnp.where(iota((8, 128), 0) == 6, peak, flipped)


def grad_kernel(width, scal, every, t_ref, s_ref, sampled, total, left, right):
    e = every[...]
    most = jnp.max(e, axis=0)
    t_top, s_top, peak = most[0:1], most[1:2], most[6:7]
    t_scale = jnp.exp(e[:, 0:1] - t_top[None])
    s_scale = jnp.exp(e[:, 1:2] - s_top[None])
    t_total = jnp.sum(e[:, 2:3] * t_scale, axis=0)
    s_total = jnp.sum(e[:, 3:4] * s_scale, axis=0)
    cross = jnp.sum(e[:, 4:5] * t_scale, axis=0)
    picked = jnp.sum(e[:, 5:6], axis=0)
    t_lse = t_top + jnp.log(t_total)
    s_lse = s_top + jnp.log(s_total)
    per_row = cross / t_total - t_lse + 2.0 * s_lse - picked
    first = scal[0] * GROUP
    count = total[0:1, 0:1].astype(jnp.int32)
    lane = iota((1, 128), 1)
    live = (lane < GROUP) & (lane + first < count)
    part = jnp.sum(jnp.where(live, per_row, 0.0), axis=1, keepdims=True)
    line = iota((8, 128), 0)
    turned = jnp.where(line == 0, t_lse, s_lse).T
    t_col, s_col = turned[:GROUP, 0:1], turned[:GROUP, 1:2]
    t, s = t_ref[...], s_ref[...]
    column = iota(t.shape, 1)
    onehot = (column + scal[2] == sampled[:, 0:1].astype(jnp.int32)).astype(F32)
    grad = 2.0 * jnp.exp(s - s_col) - jnp.exp(t - t_col) - onehot
    keep = (column < width) & (iota(t.shape, 0) + first < count)
    grad = jnp.where(keep, grad, 0.0)
    left[...] = grad[:, :LEFT].astype(BF16)
    right[...] = grad[:, LEFT:].astype(BF16)
    spare = width - LEFT
    block = spare // 128 * 128
    line, lane = iota((16, 128), 0), iota((16, 128), 1) + block - spare
    tail = grad[:16, LEFT + block : LEFT + block + 128]
    for k, value in enumerate((part, jnp.max(peak, keepdims=True))):
        for piece in range(3):
            rounded = value.astype(BF16).astype(F32)
            tail = jnp.where((line == 0) & (lane == 3 * k + piece), rounded, tail)
            value = value - rounded
    right[:16, block : block + 128] = tail.astype(BF16)


def back_kernel(
    width, half, scal, a0, b0, a1, b1, a2, b2, a3, b3, total, back_own, back_other, head,
    mine, theirs, loss, fits, grads,
):
    full = padded(width)
    for k, (a, b) in enumerate(((a0, b0), (a1, b1), (a2, b2), (a3, b3))):
        grads[k * GROUP : (k + 1) * GROUP, :LEFT] = a[...]
        grads[k * GROUP : (k + 1) * GROUP, LEFT:full] = b[...]
    x = jnp.zeros((LIVE, 2 * half), F32)
    for start in range(0, width, BLOCK):
        stop = min(start + BLOCK, width)
        x += jnp.dot(grads[:, start:stop], head[start:stop], preferred_element_type=F32)
    high = x.astype(BF16)
    low = (x - high.astype(F32)).astype(BF16)
    for back, out in ((back_own, mine), (back_other, theirs)):
        y = jnp.zeros(out.shape, F32)
        for k in (0, 1):
            cut = slice(k * half, (k + 1) * half)
            y += jnp.dot(back[k], high[:, cut], preferred_element_type=F32)
            y += jnp.dot(back[k], low[:, cut], preferred_element_type=F32)
        out[...] = y
    spare = width - LEFT
    block = spare // 128 * 128
    line, lane = iota((16, 128), 0), iota((16, 128), 1) + block - spare
    parts, peaks = [], []
    for b in (b0, b1, b2, b3):
        tail = jnp.where(line == 0, b[:16, block : block + 128].astype(F32), 0.0)
        parts.append(jnp.sum(jnp.where((lane >= 0) & (lane < 3), tail, 0.0), keepdims=True))
        peaks.append(jnp.sum(jnp.where((lane >= 3) & (lane < 6), tail, 0.0), keepdims=True))
    count = total[0:1, 0:1]
    value = ((parts[0] + parts[2]) + (parts[1] + parts[3])) / count
    peak = jnp.maximum(jnp.maximum(peaks[0], peaks[1]), jnp.maximum(peaks[2], peaks[3]))
    good = jnp.where((count <= LIVE) & (peak < BOUND), 1.0, 0.0)
    loss[0, 0] = jnp.sum(value)
    fits[0, 0] = jnp.sum(good).astype(jnp.int32)


def hidden_grad(scal, pieces, total, backs, head_t):
    width, depth = head_t.shape
    outs = (struct((ROWS, depth // 2), F32),) * 2 + (
        struct((1, 1), F32),
        struct((1, 1), jnp.int32),
    )
    return call(
        functools.partial(back_kernel, width, depth // 2),
        outs, scal, *pieces, total, *backs, head_t,
        scratch=[pltpu.VMEM((LIVE, padded(width)), BF16)],
        scalars=2,
    )


def final_kernel(scal, got, out, square):
    total = jnp.sum(got[...], axis=0)
    half = total.shape[1]
    for row in range(4):
        for k in (0, 1):
            square[row : row + 1, k * half : (k + 1) * half] = total[2 * row + k : 2 * row + k + 1]
    out[...] = square[...].astype(BF16)


def pack_kernel(ids, valid, teacher, student, out):
    dt, ds = teacher.shape[1] // 2, student.shape[1] // 2
    line = iota((8, dt), 0)
    t = jnp.zeros((8, dt), F32)
    for row in range(4):
        for k in (0, 1):
            t = jnp.where(line == 2 * row + k, teacher[row : row + 1, k * dt : (k + 1) * dt].astype(F32), t)
    out[:, :, :dt] = jnp.broadcast_to(t.astype(BF16)[None], (32, 8, dt))
    line = iota((8, ds), 0)
    s = jnp.zeros((8, ds), F32)
    for row in range(4):
        for k in (0, 1):
            s = jnp.where(line == 2 * row + k, student[row : row + 1, k * ds : (k + 1) * ds].astype(F32), s)
    out[:, :, dt + 128 :] = jnp.broadcast_to(s.astype(BF16)[None], (32, 8, ds))
    line, lane = iota((8, 128), 0), iota((8, 128), 1)
    labels = jnp.zeros((8, 128), jnp.int32)
    for row in range(4):
        token = ids[row]
        for k, value in enumerate((token & 255, (token >> 8) & 255, token >> 16, valid[row])):
            labels = jnp.where((line == 2 * row) & (lane == k), value, labels)
    out[:, :, dt : dt + 128] = jnp.broadcast_to(labels.astype(F32).astype(BF16)[None], (32, 8, 128))


def hop(x, by):
    return lax.ppermute(x, "t", [(i, (i + by) % 4) for i in range(4)])


def swap_cores(x):
    return lax.ppermute(x, "c", [(0, 1), (1, 0)])


def spread(x, axes, n):
    return lax.all_to_all(
        jnp.broadcast_to(x[None], (n,) + x.shape), axes, split_axis=0, concat_axis=0, tiled=True
    )


def short_way(teacher_hidden, student_hidden, teacher_head, student_head, token_ids, valid):
    dt, ds = teacher_hidden.shape[1], student_hidden.shape[1]
    width = teacher_head.shape[1]
    full = padded(width)
    scal = jnp.stack(
        [lax.axis_index("t"), lax.axis_index("c"), lax.axis_index(VOCAB) * width]
    ).astype(jnp.int32)
    packed = pl.pallas_call(
        pack_kernel,
        out_shape=struct((32, 8, dt // 2 + 128 + ds // 2), BF16),
        in_specs=[SMEM, SMEM, VMEM, VMEM],
        out_specs=VMEM,
    )(token_ids, valid, teacher_hidden, student_hidden)
    own = lax.all_to_all(packed, CHIPS, split_axis=0, concat_axis=0, tiled=True)
    own = own.reshape(ROWS, packed.shape[2])
    other = swap_cores(own)
    pick_own, pick_other, back_own, back_other, sampled, total = call(
        functools.partial(order_kernel, dt // 2),
        (struct((2, LIVE, ROWS), BF16),) * 2
        + (struct((2, ROWS, LIVE), BF16),) * 2
        + (struct((GROUP, 128), F32), struct((8, 128), F32)),
        scal, own, other,
    )
    sums, peaks = [], []
    for head, at, near, relayed, by in (
        (teacher_head, 0, 3, 1, 1),
        (student_head, dt // 2 + 128, 1, 3, -1),
    ):
        first, direct, mine, held, peak = partial_logits(
            scal, (pick_own, pick_other), own, other, head.T, at, near, relayed
        )
        got = hop(first, by)
        late, late_peak = call(
            relay_kernel, (struct((GROUP, full), I16), struct((8, 128), F32)), scal, got, held
        )
        sums += [mine, hop(direct, -by), hop(late, by)]
        peaks += [peak, late_peak]
    t_logits, s_logits, stats = call(
        functools.partial(stats_kernel, width),
        (struct((GROUP, full), F32),) * 2 + (struct((8, 128), F32),),
        scal, *sums, sampled, *peaks,
        scratch=[pltpu.VMEM((128, 128), F32)],
    )
    every = spread(stats, VOCAB, 64)
    a0, b0 = call(
        functools.partial(grad_kernel, width),
        (struct((GROUP, LEFT), BF16), struct((GROUP, full - LEFT), BF16)),
        scal, every, t_logits, s_logits, sampled, total,
    )
    a3, b1 = hop(a0, 1), hop(b0, -1)
    b3, a1 = hop(b0, 1), hop(a0, -1)
    a2, b2 = hop(a3, 1), hop(b1, -1)
    mine, theirs, loss, fits = hidden_grad(
        scal, (a0, b0, a1, b1, a2, b2, a3, b3), total, (back_own, back_other), student_head.T
    )
    pair = (mine + swap_cores(theirs)).reshape(32, 8, ds // 2)
    got = lax.all_to_all(pair, CHIPS, split_axis=0, concat_axis=0, tiled=True)
    (grad,) = call(
        final_kernel, (struct((4, ds), BF16),), scal, got, scratch=[pltpu.VMEM((4, ds), F32)]
    )
    return loss.reshape(()), grad, fits.reshape(()) > 0


def long_way(teacher_hidden, student_hidden, teacher_head, student_head, token_ids, valid):
    ds = student_hidden.shape[1]
    width = teacher_head.shape[1]
    group = ROWS // 4
    labels = jnp.pad(jnp.stack([token_ids, valid]), ((0, 6), (0, 124)))
    labels = spread(labels, VOCAB, 64)[:, :2, :4].transpose(1, 0, 2).reshape(2, ROWS)

    def logits(hidden, head):
        rows = spread(hidden, VOCAB, 64).reshape(ROWS, hidden.shape[1])
        part = jnp.dot(rows, head, preferred_element_type=F32).reshape(4, group, width)
        return jnp.sum(lax.all_to_all(part, "t", split_axis=0, concat_axis=0, tiled=True), axis=0)

    teacher_logits = logits(teacher_hidden, teacher_head)
    student_logits = logits(student_hidden, student_head)
    here = lax.dynamic_slice_in_dim(labels, lax.axis_index("t") * group, group, 1)
    sampled, mask = here[0], here[1].astype(F32)
    columns = lax.axis_index(VOCAB) * width + jnp.arange(width, dtype=jnp.int32)
    onehot = columns[None, :] == sampled[:, None]
    t_top = jnp.max(teacher_logits, axis=1)
    s_top = jnp.max(student_logits, axis=1)
    t_exp = jnp.exp(teacher_logits - t_top[:, None])
    s_exp = jnp.exp(student_logits - s_top[:, None])
    stats = jnp.stack(
        [
            t_top,
            s_top,
            jnp.sum(t_exp, axis=1),
            jnp.sum(s_exp, axis=1),
            jnp.sum(t_exp * (teacher_logits - student_logits), axis=1),
            jnp.sum(jnp.where(onehot, student_logits, F32(0.0)), axis=1),
        ]
    )
    every = spread(jnp.pad(stats, ((0, 2), (0, 128 - group))), VOCAB, 64)[:, :, :group]
    teacher_top = jnp.max(every[:, 0], axis=0)
    student_top = jnp.max(every[:, 1], axis=0)
    t_scale = jnp.exp(every[:, 0] - teacher_top)
    s_scale = jnp.exp(every[:, 1] - student_top)
    teacher_total = jnp.sum(every[:, 2] * t_scale, axis=0)
    student_total = jnp.sum(every[:, 3] * s_scale, axis=0)
    cross_term = jnp.sum(every[:, 4] * t_scale, axis=0)
    picked = jnp.sum(every[:, 5], axis=0)
    teacher_lse = teacher_top + jnp.log(teacher_total)
    student_lse = student_top + jnp.log(student_total)
    per_row = cross_term / teacher_total - teacher_lse + 2.0 * student_lse - picked
    loss = lax.psum(jnp.sum(mask * per_row), "t") / jnp.sum(labels[1]).astype(F32)
    teacher_prob = jnp.exp(teacher_logits - teacher_lse[:, None])
    student_prob = jnp.exp(student_logits - student_lse[:, None])
    logit_grad = (
        mask[:, None] * (2.0 * student_prob - teacher_prob - onehot.astype(F32))
    ).astype(BF16)
    part = lax.dot_general(
        lax.all_gather(logit_grad, "t", axis=0, tiled=True), student_head, NT,
        preferred_element_type=F32,
    )
    got = lax.all_to_all(part.reshape(64, 4, ds), VOCAB, split_axis=0, concat_axis=0, tiled=True)
    return loss, jnp.sum(got, axis=0).astype(BF16)


def on_device(*args):
    loss, grad, fits = short_way(*args)
    return lax.cond(fits, lambda *_: (loss, grad), long_way, *args)


def solution(mesh):
    fine = Mesh(mesh.devices.reshape(4, 4, 2, 2, 4), VOCAB + ("t",))
    in_specs = (
        P(VOCAB, "t"),
        P(VOCAB, "t"),
        P("t", VOCAB),
        P("t", VOCAB),
        P(VOCAB),
        P(VOCAB),
    )
    return jax.shard_map(
        on_device, mesh=fine, in_specs=in_specs, out_specs=(P(), P(VOCAB, "t")), check_vma=False
    )
```

```python
import functools

import jax
import jax.numpy as jnp
from jax import lax
from jax.experimental import pallas as pl
from jax.experimental.pallas import tpu as pltpu
from jax.sharding import Mesh, PartitionSpec as P

VOCAB = ("y", "x", "zl", "c")
CHIPS = ("y", "x", "zl")
ROWS = 256
LIVE = 192
GROUP = LIVE // 4
LEFT = 1280
BLOCK = 512
STEP = 1024.0
BOUND = 31.9
F32 = jnp.float32
BF16 = jnp.bfloat16
I16 = jnp.int16
NT = (((1,), (1,)), ((), ()))
VMEM = pl.BlockSpec(memory_space=pltpu.VMEM)
SMEM = pl.BlockSpec(memory_space=pltpu.SMEM)
ANY = pl.BlockSpec(memory_space=pl.ANY)


def struct(shape, dtype):
    return jax.ShapeDtypeStruct(shape, dtype)


def call(body, outs, *args, scratch=(), scalars=0, streamed=0):
    return pl.pallas_call(
        body,
        out_shape=outs,
        in_specs=[SMEM] + [VMEM] * (len(args) - 1 - streamed) + [ANY] * streamed,
        out_specs=[VMEM] * (len(outs) - scalars) + [SMEM] * scalars,
        scratch_shapes=scratch,
        compiler_params=pltpu.CompilerParams(vmem_limit_bytes=32 << 20),
    )(*args)


def padded(width):
    return -(-width // 128) * 128


def coded(x):
    return jnp.clip(jnp.round(x * STEP), -32767.0, 32767.0).astype(jnp.int32).astype(I16)


def decoded(x):
    return x.astype(jnp.int32).astype(F32) * (1.0 / STEP)


def iota(shape, axis):
    return lax.broadcasted_iota(jnp.int32, shape, axis)


def order(scal, own, other, at, pick_own, pick_other, back_own, back_other, sampled, total):
    me, core = scal[0], scal[1].astype(F32)
    wide = own.shape[0]
    line, lane = iota((wide, wide), 0), iota((wide, wide), 1)
    even = lane - lane % 2
    before = (line < even).astype(F32).astype(BF16)
    same = (line == even).astype(F32).astype(BF16)
    found = []
    for ref in (own, other):
        labels = ref[:, at : at + 128].astype(F32).T[:8].astype(BF16)
        earlier = jnp.dot(labels, before, preferred_element_type=F32)[3:4]
        here = jnp.dot(labels, same, preferred_element_type=F32)
        ids = here[0:1] + 256.0 * here[1:2] + 65536.0 * here[2:3]
        found.append((here[3:4] > 0.5, earlier, ids, 0.5 * jnp.sum(here[3:4], keepdims=True)))
    start = (core * found[1][3], (1.0 - core) * found[0][3])
    shift = (me * GROUP).astype(F32)
    picked = jnp.zeros((GROUP, 1), F32)
    for (ok, earlier, ids, _), base, pick, back in zip(
        found, start, (pick_own, pick_other), (back_own, back_other)
    ):
        slot = base + earlier
        near = slot - shift
        near = jnp.where(near < 0.0, near + LIVE, near)
        near = jnp.where(ok & (slot < LIVE), near, -1.0)
        column = jnp.broadcast_to(near, (8, wide)).T[:, 0:1]
        row = iota((LIVE, wide), 0).astype(F32)
        odd = iota((LIVE, wide), 1) % 2
        hit = row == near
        slots = iota((wide, LIVE), 1).astype(F32)
        turn = iota((wide, LIVE), 0) % 2
        back_hit = slots == column
        for half in (0, 1):
            pick[half] = (hit & (odd == half)).astype(F32).astype(BF16)
            back[half] = (back_hit & (turn == half)).astype(F32).astype(BF16)
        chosen = (hit & (odd == 0))[:GROUP]
        picked += jnp.sum(jnp.where(chosen, ids, 0.0), axis=1, keepdims=True)
    sampled[...] = jnp.broadcast_to(picked, sampled.shape)
    total[...] = jnp.broadcast_to(found[0][3] + found[1][3], total.shape)


def front_kernel(
    width, places, scal, own, other, t_head, s_head,
    back_own, back_other, sampled, total,
    t_first, t_direct, t_mine, t_held, t_peak, s_first, s_direct, s_mine, s_held, s_peak,
    pick_own, pick_other, t_rows, s_rows, t_loaded, s_loaded, logits, sems,
):
    full = padded(width)
    edge = full - 128
    g = GROUP
    blocks = [(start, min(start + BLOCK, width)) for start in range(0, width, BLOCK)]
    copies = [
        [
            pltpu.make_async_copy(
                head.at[start:stop], loaded.at[start:stop], sems.at[k * len(blocks) + n]
            )
            for n, (start, stop) in enumerate(blocks)
        ]
        for k, (head, loaded) in enumerate(((t_head, t_loaded), (s_head, s_loaded)))
    ]
    for copy in copies[0] + copies[1]:
        copy.start()
    order(
        scal, own, other, t_rows.shape[1] // 2,
        pick_own, pick_other, back_own, back_other, sampled, total,
    )
    logits[:, edge:full] = jnp.zeros((LIVE, 128), F32)
    for (at, near, relayed), waits, rows, loaded, (first, direct, mine, held, peak) in zip(
        places,
        copies,
        (t_rows, s_rows),
        (t_loaded, s_loaded),
        ((t_first, t_direct, t_mine, t_held, t_peak), (s_first, s_direct, s_mine, s_held, s_peak)),
    ):
        half = rows.shape[1] // 2
        for k in (0, 1):
            rows[:, k * half : (k + 1) * half] = (
                jnp.dot(pick_own[k], own[:, at : at + half], preferred_element_type=F32)
                + jnp.dot(pick_other[k], other[:, at : at + half], preferred_element_type=F32)
            ).astype(BF16)
        for (start, stop), wait in zip(blocks, waits):
            wait.wait()
            logits[:, start:stop] = lax.dot_general(
                rows[...], loaded[start:stop], NT, preferred_element_type=F32
            )
        first[...] = coded(logits[2 * g : 3 * g])
        direct[...] = coded(logits[near * g : (near + 1) * g])
        mine[...] = logits[:g]
        held[...] = logits[relayed * g : (relayed + 1) * g]
        peak[...] = jnp.broadcast_to(jnp.max(jnp.abs(logits[g:]), keepdims=True), peak.shape)


def relay_kernel(scal, got, held, out, peak):
    total = held[...] + decoded(got[...])
    out[...] = coded(total)
    peak[...] = jnp.broadcast_to(jnp.max(jnp.abs(total), keepdims=True), peak.shape)


def stats_kernel(
    width, scal, t_mine, t_direct, t_late, s_mine, s_direct, s_late, sampled, p0, p1, p2, p3,
    t_out, s_out, stats, square,
):
    t = t_mine[...] + decoded(t_direct[...]) + decoded(t_late[...])
    s = s_mine[...] + decoded(s_direct[...]) + decoded(s_late[...])
    t_out[...] = t
    s_out[...] = s
    column = iota(t.shape, 1)
    inside = column < width
    onehot = (column + scal[2] == sampled[:, 0:1].astype(jnp.int32)) & inside
    t_top = jnp.max(jnp.where(inside, t, -jnp.inf), axis=1, keepdims=True)
    s_top = jnp.max(jnp.where(inside, s, -jnp.inf), axis=1, keepdims=True)
    t_exp = jnp.where(inside, jnp.exp(t - t_top), 0.0)
    s_exp = jnp.where(inside, jnp.exp(s - s_top), 0.0)
    values = (
        t_top,
        s_top,
        jnp.sum(t_exp, axis=1, keepdims=True),
        jnp.sum(s_exp, axis=1, keepdims=True),
        jnp.sum(t_exp * (t - s), axis=1, keepdims=True),
        jnp.sum(jnp.where(onehot, s, 0.0), axis=1, keepdims=True),
    )
    lane = iota((GROUP, 128), 1)
    board = jnp.zeros((GROUP, 128), F32)
    for k, value in enumerate(values):
        board = jnp.where(lane == k, value, board)
    square[...] = jnp.zeros(square.shape, F32)
    square[:GROUP] = board
    flipped = square[...].T[:8]
    peak = jnp.maximum(jnp.maximum(p0[...], p1[...]), jnp.maximum(p2[...], p3[...]))
    stats[...] = jnp.where(iota((8, 128), 0) == 6, peak, flipped)


def grad_kernel(width, scal, every, t_ref, s_ref, sampled, total, left, right):
    e = every[...]
    most = jnp.max(e, axis=0)
    t_top, s_top, peak = most[0:1], most[1:2], most[6:7]
    t_scale = jnp.exp(e[:, 0:1] - t_top[None])
    s_scale = jnp.exp(e[:, 1:2] - s_top[None])
    t_total = jnp.sum(e[:, 2:3] * t_scale, axis=0)
    s_total = jnp.sum(e[:, 3:4] * s_scale, axis=0)
    cross = jnp.sum(e[:, 4:5] * t_scale, axis=0)
    picked = jnp.sum(e[:, 5:6], axis=0)
    t_lse = t_top + jnp.log(t_total)
    s_lse = s_top + jnp.log(s_total)
    per_row = cross / t_total - t_lse + 2.0 * s_lse - picked
    first = scal[0] * GROUP
    count = total[0:1, 0:1].astype(jnp.int32)
    lane = iota((1, 128), 1)
    live = (lane < GROUP) & (lane + first < count)
    part = jnp.sum(jnp.where(live, per_row, 0.0), axis=1, keepdims=True)
    line = iota((8, 128), 0)
    turned = jnp.where(line == 0, t_lse, s_lse).T
    t_col, s_col = turned[:GROUP, 0:1], turned[:GROUP, 1:2]
    t, s = t_ref[...], s_ref[...]
    column = iota(t.shape, 1)
    onehot = (column + scal[2] == sampled[:, 0:1].astype(jnp.int32)).astype(F32)
    grad = 2.0 * jnp.exp(s - s_col) - jnp.exp(t - t_col) - onehot
    keep = (column < width) & (iota(t.shape, 0) + first < count)
    grad = jnp.where(keep, grad, 0.0)
    left[...] = grad[:, :LEFT].astype(BF16)
    right[...] = grad[:, LEFT:].astype(BF16)
    block = width // 128 * 128
    line, lane = iota((16, 128), 0), iota((16, 128), 1) + block - width
    tail = grad[:16, block : block + 128]
    for k, value in enumerate((part, jnp.max(peak, keepdims=True))):
        for piece in range(3):
            rounded = value.astype(BF16).astype(F32)
            tail = jnp.where((line == 0) & (lane == 3 * k + piece), rounded, tail)
            value = value - rounded
    right[:16, block - LEFT : block - LEFT + 128] = tail.astype(BF16)


def back_kernel(
    width, half, scal, a0, b0, a1, b1, a2, b2, a3, b3, total, back_own, back_other, head,
    mine, theirs, loss, fits, grads,
):
    for k, (a, b) in enumerate(((a0, b0), (a1, b1), (a2, b2), (a3, b3))):
        grads[k * GROUP : (k + 1) * GROUP, :LEFT] = a[...]
        grads[k * GROUP : (k + 1) * GROUP, LEFT:] = b[...]
    x = jnp.zeros((LIVE, 2 * half), F32)
    for start in range(0, width, BLOCK):
        stop = min(start + BLOCK, width)
        x += jnp.dot(grads[:, start:stop], head[start:stop], preferred_element_type=F32)
    high = x.astype(BF16)
    low = (x - high.astype(F32)).astype(BF16)
    for back, out in ((back_own, mine), (back_other, theirs)):
        y = jnp.zeros(out.shape, F32)
        for k in (0, 1):
            cut = slice(k * half, (k + 1) * half)
            y += jnp.dot(back[k], high[:, cut], preferred_element_type=F32)
            y += jnp.dot(back[k], low[:, cut], preferred_element_type=F32)
        out[...] = y
    block = width // 128 * 128
    line, lane = iota((16, 128), 0), iota((16, 128), 1) + block - width
    block -= LEFT
    parts, peaks = [], []
    for ref in (b0, b1, b2, b3):
        tail = jnp.where(line == 0, ref[:16, block : block + 128].astype(F32), 0.0)
        parts.append(jnp.sum(jnp.where((lane >= 0) & (lane < 3), tail, 0.0), keepdims=True))
        peaks.append(jnp.sum(jnp.where((lane >= 3) & (lane < 6), tail, 0.0), keepdims=True))
    count = total[0:1, 0:1]
    value = ((parts[0] + parts[2]) + (parts[1] + parts[3])) / count
    peak = jnp.maximum(jnp.maximum(peaks[0], peaks[1]), jnp.maximum(peaks[2], peaks[3]))
    good = jnp.where((count <= LIVE) & (peak < BOUND), 1.0, 0.0)
    loss[0, 0] = jnp.sum(value)
    fits[0, 0] = jnp.sum(good).astype(jnp.int32)


def hidden_grad(scal, a0, b0, total, backs, head_t):
    width, depth = head_t.shape
    full = padded(width)
    a3, b1 = hop(a0, 1), hop(b0, -1)
    b3, a1 = hop(b0, 1), hop(a0, -1)
    a2, b2 = hop(a3, 1), hop(b1, -1)
    outs = (struct((ROWS, depth // 2), F32),) * 2 + (
        struct((1, 1), F32),
        struct((1, 1), jnp.int32),
    )
    return call(
        functools.partial(back_kernel, width, depth // 2),
        outs, scal, a0, b0, a1, b1, a2, b2, a3, b3, total, *backs, head_t,
        scratch=[pltpu.VMEM((LIVE, full), BF16)],
        scalars=2,
    )


def pair_kernel(scal, mine, theirs, out):
    x = mine[...] + theirs[...]
    top = jnp.maximum(jnp.max(jnp.abs(x), axis=1, keepdims=True), 1e-30)
    power = jnp.ceil(jnp.log2(top) + 0.001)
    codes = jnp.round(x * jnp.exp2(15.0 - power))
    half = x.shape[1]
    out[:, :half] = jnp.clip(codes, -32767.0, 32767.0).astype(jnp.int32).astype(I16)
    out[:, half:] = jnp.broadcast_to(power, (x.shape[0], 128)).astype(jnp.int32).astype(I16)


def final_kernel(scal, got, out, square):
    half = got.shape[2] - 128
    total = jnp.zeros((8, half), F32)
    for chip in range(got.shape[0]):
        power = got[chip, :, half : half + 128].astype(jnp.int32).astype(F32)[:, 0:1]
        total += got[chip, :, :half].astype(jnp.int32).astype(F32) * jnp.exp2(power - 15.0)
    for row in range(4):
        for k in (0, 1):
            square[row : row + 1, k * half : (k + 1) * half] = total[2 * row + k : 2 * row + k + 1]
    out[...] = square[...].astype(BF16)


def pack_kernel(ids, valid, teacher, student, out):
    dt, ds = teacher.shape[1] // 2, student.shape[1] // 2
    line = iota((8, dt), 0)
    t = jnp.zeros((8, dt), F32)
    for row in range(4):
        for k in (0, 1):
            t = jnp.where(line == 2 * row + k, teacher[row : row + 1, k * dt : (k + 1) * dt].astype(F32), t)
    out[:, :, :dt] = jnp.broadcast_to(t.astype(BF16)[None], (32, 8, dt))
    line = iota((8, ds), 0)
    s = jnp.zeros((8, ds), F32)
    for row in range(4):
        for k in (0, 1):
            s = jnp.where(line == 2 * row + k, student[row : row + 1, k * ds : (k + 1) * ds].astype(F32), s)
    out[:, :, dt + 128 :] = jnp.broadcast_to(s.astype(BF16)[None], (32, 8, ds))
    line, lane = iota((8, 128), 0), iota((8, 128), 1)
    labels = jnp.zeros((8, 128), jnp.int32)
    for row in range(4):
        token = ids[row]
        for k, value in enumerate((token & 255, (token >> 8) & 255, token >> 16, valid[row])):
            labels = jnp.where((line == 2 * row) & (lane == k), value, labels)
    out[:, :, dt : dt + 128] = jnp.broadcast_to(labels.astype(F32).astype(BF16)[None], (32, 8, 128))


def hop(x, by):
    return lax.ppermute(x, "t", [(i, (i + by) % 4) for i in range(4)])


def swap_cores(x):
    return lax.ppermute(x, "c", [(0, 1), (1, 0)])


def spread(x, axes, n):
    return lax.all_to_all(
        jnp.broadcast_to(x[None], (n,) + x.shape), axes, split_axis=0, concat_axis=0, tiled=True
    )


def short_way(teacher_hidden, student_hidden, teacher_head, student_head, token_ids, valid):
    dt, ds = teacher_hidden.shape[1], student_hidden.shape[1]
    width = teacher_head.shape[1]
    full = padded(width)
    scal = jnp.stack(
        [lax.axis_index("t"), lax.axis_index("c"), lax.axis_index(VOCAB) * width]
    ).astype(jnp.int32)
    packed = pl.pallas_call(
        pack_kernel,
        out_shape=struct((32, 8, dt // 2 + 128 + ds // 2), BF16),
        in_specs=[SMEM, SMEM, VMEM, VMEM],
        out_specs=VMEM,
        compiler_params=pltpu.CompilerParams(vmem_limit_bytes=8 << 20),
    )(token_ids, valid, teacher_hidden, student_hidden)
    t_head, s_head = teacher_head.T, student_head.T
    own = lax.all_to_all(packed, CHIPS, split_axis=0, concat_axis=0, tiled=True)
    own = own.reshape(ROWS, packed.shape[2])
    other = swap_cores(own)
    one = (
        struct((GROUP, full), I16),
        struct((GROUP, full), I16),
        struct((GROUP, full), F32),
        struct((GROUP, full), F32),
        struct((8, 128), F32),
    )
    back_own, back_other, sampled, total, *made = call(
        functools.partial(front_kernel, width, ((0, 3, 1), (dt // 2 + 128, 1, 3))),
        (struct((2, ROWS, LIVE), BF16),) * 2
        + (struct((GROUP, 128), F32), struct((8, 128), F32))
        + one + one,
        scal, own, other, t_head, s_head,
        scratch=[
            pltpu.VMEM((2, LIVE, ROWS), BF16),
            pltpu.VMEM((2, LIVE, ROWS), BF16),
            pltpu.VMEM((LIVE, dt), BF16),
            pltpu.VMEM((LIVE, ds), BF16),
            pltpu.VMEM(t_head.shape, BF16),
            pltpu.VMEM(s_head.shape, BF16),
            pltpu.VMEM((LIVE, full), F32),
            pltpu.SemaphoreType.DMA((2 * pl.cdiv(width, BLOCK),)),
        ],
        streamed=2,
    )
    sums, peaks = [], []
    for (first, direct, mine, held, peak), by in ((made[:5], 1), (made[5:], -1)):
        late, late_peak = call(
            relay_kernel,
            (struct((GROUP, full), I16), struct((8, 128), F32)),
            scal, hop(first, by), held,
        )
        sums += [mine, hop(direct, -by), hop(late, by)]
        peaks += [peak, late_peak]
    t_logits, s_logits, stats = call(
        functools.partial(stats_kernel, width),
        (struct((GROUP, full), F32),) * 2 + (struct((8, 128), F32),),
        scal, *sums, sampled, *peaks,
        scratch=[pltpu.VMEM((128, 128), F32)],
    )
    every = spread(stats, VOCAB, 64)
    a0, b0 = call(
        functools.partial(grad_kernel, width),
        (struct((GROUP, LEFT), BF16), struct((GROUP, full - LEFT), BF16)),
        scal, every, t_logits, s_logits, sampled, total,
    )
    mine, theirs, loss, fits = hidden_grad(
        scal, a0, b0, total, (back_own, back_other), s_head
    )
    (pair,) = call(
        pair_kernel, (struct((ROWS, ds // 2 + 128), I16),), scal, mine, swap_cores(theirs)
    )
    pair = pair.reshape(32, 8, ds // 2 + 128)
    got = lax.all_to_all(pair, CHIPS, split_axis=0, concat_axis=0, tiled=True)
    (grad,) = call(
        final_kernel, (struct((4, ds), BF16),), scal, got, scratch=[pltpu.VMEM((4, ds), F32)]
    )
    return loss.reshape(()), grad, fits.reshape(()) > 0


def long_way(teacher_hidden, student_hidden, teacher_head, student_head, token_ids, valid):
    ds = student_hidden.shape[1]
    width = teacher_head.shape[1]
    group = ROWS // 4
    labels = jnp.pad(jnp.stack([token_ids, valid]), ((0, 6), (0, 124)))
    labels = spread(labels, VOCAB, 64)[:, :2, :4].transpose(1, 0, 2).reshape(2, ROWS)

    def logits(hidden, head):
        rows = spread(hidden, VOCAB, 64).reshape(ROWS, hidden.shape[1])
        part = jnp.dot(rows, head, preferred_element_type=F32).reshape(4, group, width)
        return jnp.sum(lax.all_to_all(part, "t", split_axis=0, concat_axis=0, tiled=True), axis=0)

    teacher_logits = logits(teacher_hidden, teacher_head)
    student_logits = logits(student_hidden, student_head)
    here = lax.dynamic_slice_in_dim(labels, lax.axis_index("t") * group, group, 1)
    sampled, mask = here[0], here[1].astype(F32)
    columns = lax.axis_index(VOCAB) * width + jnp.arange(width, dtype=jnp.int32)
    onehot = columns[None, :] == sampled[:, None]
    t_top = jnp.max(teacher_logits, axis=1)
    s_top = jnp.max(student_logits, axis=1)
    t_exp = jnp.exp(teacher_logits - t_top[:, None])
    s_exp = jnp.exp(student_logits - s_top[:, None])
    stats = jnp.stack(
        [
            t_top,
            s_top,
            jnp.sum(t_exp, axis=1),
            jnp.sum(s_exp, axis=1),
            jnp.sum(t_exp * (teacher_logits - student_logits), axis=1),
            jnp.sum(jnp.where(onehot, student_logits, F32(0.0)), axis=1),
        ]
    )
    every = spread(jnp.pad(stats, ((0, 2), (0, 128 - group))), VOCAB, 64)[:, :, :group]
    teacher_top = jnp.max(every[:, 0], axis=0)
    student_top = jnp.max(every[:, 1], axis=0)
    t_scale = jnp.exp(every[:, 0] - teacher_top)
    s_scale = jnp.exp(every[:, 1] - student_top)
    teacher_total = jnp.sum(every[:, 2] * t_scale, axis=0)
    student_total = jnp.sum(every[:, 3] * s_scale, axis=0)
    cross_term = jnp.sum(every[:, 4] * t_scale, axis=0)
    picked = jnp.sum(every[:, 5], axis=0)
    teacher_lse = teacher_top + jnp.log(teacher_total)
    student_lse = student_top + jnp.log(student_total)
    per_row = cross_term / teacher_total - teacher_lse + 2.0 * student_lse - picked
    parts = spread(jnp.full((8, 128), jnp.sum(mask * per_row)), "t", 4)[:, 0, 0]
    loss = jnp.sum(parts) / jnp.sum(labels[1]).astype(F32)
    teacher_prob = jnp.exp(teacher_logits - teacher_lse[:, None])
    student_prob = jnp.exp(student_logits - student_lse[:, None])
    logit_grad = (
        mask[:, None] * (2.0 * student_prob - teacher_prob - onehot.astype(F32))
    ).astype(BF16)
    part = lax.dot_general(
        spread(logit_grad, "t", 4).reshape(ROWS, width), student_head, NT,
        preferred_element_type=F32,
    )
    got = lax.all_to_all(part.reshape(64, 4, ds), VOCAB, split_axis=0, concat_axis=0, tiled=True)
    return loss, jnp.sum(got, axis=0).astype(BF16)


def on_device(*args):
    loss, grad, fits = short_way(*args)
    return lax.cond(fits, lambda *_: (loss, grad), long_way, *args)


def solution(mesh):
    fine = Mesh(mesh.devices.reshape(4, 4, 2, 2, 4), VOCAB + ("t",))
    in_specs = (
        P(VOCAB, "t"),
        P(VOCAB, "t"),
        P("t", VOCAB),
        P("t", VOCAB),
        P(VOCAB),
        P(VOCAB),
    )
    return jax.shard_map(
        on_device, mesh=fine, in_specs=in_specs, out_specs=(P(), P(VOCAB, "t")), check_vma=False
    )
```

```python
import functools

import jax
import jax.numpy as jnp
from jax import lax
from jax.experimental import pallas as pl
from jax.experimental.pallas import tpu as pltpu
from jax.sharding import Mesh, PartitionSpec as P

VOCAB = ("y", "x", "zl", "c")
CHIPS = ("y", "x", "zl")
ROWS = 256
LIVE = 192
GROUP = LIVE // 4
LEFT = 1280
STEP = 1024.0
BOUND = 31.9
ROUND = 1.5 * 2.0**23
F32 = jnp.float32
BF16 = jnp.bfloat16
I16 = jnp.int16
NT = (((1,), (1,)), ((), ()))
VMEM = pl.BlockSpec(memory_space=pltpu.VMEM)
SMEM = pl.BlockSpec(memory_space=pltpu.SMEM)
ANY = pl.BlockSpec(memory_space=pl.ANY)


def struct(shape, dtype):
    return jax.ShapeDtypeStruct(shape, dtype)


def call(body, outs, *args, scratch=(), scalars=0, streamed=0):
    return pl.pallas_call(
        body,
        out_shape=outs,
        in_specs=[SMEM] + [VMEM] * (len(args) - 1 - streamed) + [ANY] * streamed,
        out_specs=[VMEM] * (len(outs) - scalars) + [SMEM] * scalars,
        scratch_shapes=scratch,
        compiler_params=pltpu.CompilerParams(vmem_limit_bytes=32 << 20),
    )(*args)


def padded(width):
    return -(-width // 128) * 128


def coded(x):
    return ((x * STEP + ROUND) - ROUND).astype(jnp.int32).astype(I16)


def decoded(x):
    return x.astype(jnp.int32).astype(F32) * (1.0 / STEP)


def iota(shape, axis):
    return lax.broadcasted_iota(jnp.int32, shape, axis)


def order(scal, own, other, at, pick_own, pick_other, back_own, back_other, sampled, total):
    me, core = scal[0], scal[1].astype(F32)
    wide = own.shape[0]
    line, lane = iota((wide, wide), 0), iota((wide, wide), 1)
    even = lane - lane % 2
    before = (line < even).astype(F32).astype(BF16)
    same = (line == even).astype(F32).astype(BF16)
    evens = (iota((wide, wide // 2), 0) == 2 * iota((wide, wide // 2), 1)).astype(F32).astype(BF16)
    found = []
    for ref in (own, other):
        labels = ref[:, at : at + 128].astype(F32).T[:8].astype(BF16)
        earlier = jnp.dot(labels, before, preferred_element_type=F32)[3:4]
        here = jnp.dot(labels, same, preferred_element_type=F32)
        ids = here[0:1] + 256.0 * here[1:2] + 65536.0 * here[2:3]
        found.append((here[3:4] > 0.5, earlier, ids, 0.5 * jnp.sum(here[3:4], keepdims=True)))
    start = (core * found[1][3], (1.0 - core) * found[0][3])
    picked = jnp.zeros((GROUP, 1), F32)
    for (ok, earlier, ids, _), base, pick, back in zip(
        found, start, (pick_own, pick_other), (back_own, back_other)
    ):
        slot = base + earlier
        group = jnp.floor(slot * (1.0 / GROUP) + 1e-3)
        turn = (group - me.astype(F32)) * (1.0 - 2.0 * core)
        turn = jnp.where(turn < 0.0, turn + 4.0, turn)
        near = slot + GROUP * (turn - group)
        near = jnp.where(ok & (slot < LIVE), near, -1.0)
        column = jnp.dot(
            jnp.broadcast_to(near, (8, wide)).astype(BF16), evens, preferred_element_type=F32
        ).T[:, 0:1]
        row = iota((LIVE, wide), 0).astype(F32)
        odd = iota((LIVE, wide), 1) % 2
        hit = row == near
        slots = (iota((wide // 2, 2 * ROWS), 1) % ROWS).astype(F32)
        back[...] = (slots == column).astype(F32).astype(BF16)
        for half in (0, 1):
            pick[half] = (hit & (odd == half)).astype(F32).astype(BF16)
        chosen = (hit & (odd == 0))[:GROUP]
        picked += jnp.sum(jnp.where(chosen, ids, 0.0), axis=1, keepdims=True)
    sampled[...] = jnp.broadcast_to(picked, sampled.shape)
    total[...] = jnp.broadcast_to(found[0][3] + found[1][3], total.shape)


def front_kernel(
    width, places, scal, own, other, t_head, s_head,
    back_own, back_other, sampled, total,
    t_first, t_direct, t_mine, t_held, t_peak, s_first, s_direct, s_mine, s_held, s_peak,
    pick_own, pick_other, t_rows, s_rows, t_loaded, s_loaded, logits, sems,
):
    full = padded(width)
    edge = full - 128
    g = GROUP
    copies = [
        pltpu.make_async_copy(head, loaded, sems.at[k])
        for k, (head, loaded) in enumerate(((t_head, t_loaded), (s_head, s_loaded)))
    ]
    for copy in copies:
        copy.start()
    order(
        scal, own, other, t_rows.shape[1] // 2,
        pick_own, pick_other, back_own, back_other, sampled, total,
    )
    logits[:, edge:full] = jnp.zeros((LIVE, 128), F32)
    for (at, near, relayed), copy, rows, loaded, (first, direct, mine, held, peak) in zip(
        places,
        copies,
        (t_rows, s_rows),
        (t_loaded, s_loaded),
        ((t_first, t_direct, t_mine, t_held, t_peak), (s_first, s_direct, s_mine, s_held, s_peak)),
    ):
        half = rows.shape[1] // 2
        for k in (0, 1):
            rows[:, k * half : (k + 1) * half] = (
                jnp.dot(pick_own[k], own[:, at : at + half], preferred_element_type=F32)
                + jnp.dot(pick_other[k], other[:, at : at + half], preferred_element_type=F32)
            ).astype(BF16)
        copy.wait()
        logits[:, :width] = lax.dot_general(
            rows[...], loaded[...], NT, preferred_element_type=F32
        )
        first[...] = coded(logits[2 * g : 3 * g])
        direct[...] = coded(logits[near * g : (near + 1) * g])
        mine[...] = logits[:g]
        held[...] = logits[relayed * g : (relayed + 1) * g]
        peak[...] = jnp.broadcast_to(jnp.max(jnp.abs(logits[g:]), keepdims=True), peak.shape)


def relay_kernel(scal, got, held, out, peak):
    total = held[...] + decoded(got[...])
    out[...] = coded(total)
    peak[...] = jnp.broadcast_to(jnp.max(jnp.abs(total), keepdims=True), peak.shape)


def stats_kernel(
    width, scal, t_mine, t_direct, t_late, s_mine, s_direct, s_late, sampled, p0, p1, p2, p3,
    t_out, s_out, stats, square,
):
    t = t_mine[...] + decoded(t_direct[...]) + decoded(t_late[...])
    s = s_mine[...] + decoded(s_direct[...]) + decoded(s_late[...])
    t_out[...] = t
    s_out[...] = s
    column = iota(t.shape, 1)
    inside = column < width
    onehot = (column + scal[2] == sampled[:, 0:1].astype(jnp.int32)) & inside
    t_top = jnp.max(jnp.where(inside, t, -jnp.inf), axis=1, keepdims=True)
    s_top = jnp.max(jnp.where(inside, s, -jnp.inf), axis=1, keepdims=True)
    t_exp = jnp.where(inside, jnp.exp(t - t_top), 0.0)
    s_exp = jnp.where(inside, jnp.exp(s - s_top), 0.0)
    values = (
        t_top,
        s_top,
        jnp.sum(t_exp, axis=1, keepdims=True),
        jnp.sum(s_exp, axis=1, keepdims=True),
        jnp.sum(t_exp * (t - s), axis=1, keepdims=True),
        jnp.sum(jnp.where(onehot, s, 0.0), axis=1, keepdims=True),
    )
    lane = iota((GROUP, 128), 1)
    board = jnp.zeros((GROUP, 128), F32)
    for k, value in enumerate(values):
        board = jnp.where(lane == k, value, board)
    square[...] = jnp.zeros(square.shape, F32)
    square[:GROUP] = board
    flipped = square[...].T[:8]
    peak = jnp.maximum(jnp.maximum(p0[...], p1[...]), jnp.maximum(p2[...], p3[...]))
    stats[...] = jnp.where(iota((8, 128), 0) == 6, peak, flipped)


def merge_kernel(scal, mine, theirs, out):
    a, b = mine[...], theirs[...]
    top = jnp.maximum(a, b)
    line = iota(a.shape, 0)
    scaled = []
    for x in (a, b):
        scale = jnp.exp(x - top)
        factor = jnp.where(line == 3, scale[1:2], jnp.where(line == 5, 1.0, scale[0:1]))
        scaled.append(x * factor)
    both = jnp.where((line < 2) | (line == 6), top, scaled[0] + scaled[1])
    out[...] = jnp.broadcast_to(both[None], out.shape)


def grad_kernel(width, scal, every, t_ref, s_ref, sampled, total, left, right):
    e = every[...]
    most = jnp.max(e, axis=0)
    t_top, s_top, peak = most[0:1], most[1:2], most[6:7]
    t_scale = jnp.exp(e[:, 0:1] - t_top[None])
    s_scale = jnp.exp(e[:, 1:2] - s_top[None])
    t_total = jnp.sum(e[:, 2:3] * t_scale, axis=0)
    s_total = jnp.sum(e[:, 3:4] * s_scale, axis=0)
    cross = jnp.sum(e[:, 4:5] * t_scale, axis=0)
    picked = jnp.sum(e[:, 5:6], axis=0)
    t_lse = t_top + jnp.log(t_total)
    s_lse = s_top + jnp.log(s_total)
    per_row = cross / t_total - t_lse + 2.0 * s_lse - picked
    first = scal[0] * GROUP
    count = total[0:1, 0:1].astype(jnp.int32)
    lane = iota((1, 128), 1)
    live = (lane < GROUP) & (lane + first < count)
    part = jnp.sum(jnp.where(live, per_row, 0.0), axis=1, keepdims=True)
    line = iota((8, 128), 0)
    turned = jnp.where(line == 0, t_lse, s_lse).T
    t_col, s_col = turned[:GROUP, 0:1], turned[:GROUP, 1:2]
    t, s = t_ref[...], s_ref[...]
    column = iota(t.shape, 1)
    onehot = (column + scal[2] == sampled[:, 0:1].astype(jnp.int32)).astype(F32)
    grad = 2.0 * jnp.exp(s - s_col) - jnp.exp(t - t_col) - onehot
    keep = (column < width) & (iota(t.shape, 0) + first < count)
    grad = jnp.where(keep, grad, 0.0)
    left[...] = grad[:, :LEFT].astype(BF16)
    right[...] = grad[:, LEFT:].astype(BF16)
    block = width // 128 * 128
    line, lane = iota((16, 128), 0), iota((16, 128), 1) + block - width
    tail = grad[:16, block : block + 128]
    for k, value in enumerate((part, jnp.max(peak, keepdims=True))):
        for piece in range(3):
            rounded = value.astype(BF16).astype(F32)
            tail = jnp.where((line == 0) & (lane == 3 * k + piece), rounded, tail)
            value = value - rounded
    right[:16, block - LEFT : block - LEFT + 128] = tail.astype(BF16)


def back_kernel(
    width, scal, a0, b0, a1, b1, a2, b2, a3, b3, total, back_own, back_other, head,
    mine, theirs, loss, fits, grads, parts,
):
    for k, (a, b) in enumerate(((a0, b0), (a1, b1), (a2, b2), (a3, b3))):
        grads[k * GROUP : (k + 1) * GROUP, :LEFT] = a[...]
        grads[k * GROUP : (k + 1) * GROUP, LEFT:] = b[...]
    x = jnp.dot(grads[:, :width], head[...], preferred_element_type=F32)
    high = x.astype(BF16)
    low = (x - high.astype(F32)).astype(BF16)
    for k, part in enumerate((high, low)):
        parts[k * ROWS : k * ROWS + LIVE] = part
        parts[k * ROWS + LIVE : (k + 1) * ROWS] = jnp.zeros((ROWS - LIVE, x.shape[1]), BF16)
    for back, out in ((back_own, mine), (back_other, theirs)):
        out[...] = jnp.dot(back[...], parts[...], preferred_element_type=F32)
    block = width // 128 * 128
    line, lane = iota((16, 128), 0), iota((16, 128), 1) + block - width
    block -= LEFT
    sums, peaks = [], []
    for ref in (b0, b1, b2, b3):
        tail = jnp.where(line == 0, ref[:16, block : block + 128].astype(F32), 0.0)
        sums.append(jnp.sum(jnp.where((lane >= 0) & (lane < 3), tail, 0.0), keepdims=True))
        peaks.append(jnp.sum(jnp.where((lane >= 3) & (lane < 6), tail, 0.0), keepdims=True))
    count = total[0:1, 0:1]
    value = ((sums[0] + sums[2]) + (sums[1] + sums[3])) / count
    peak = jnp.maximum(jnp.maximum(peaks[0], peaks[1]), jnp.maximum(peaks[2], peaks[3]))
    good = jnp.where((count <= LIVE) & (peak < BOUND), 1.0, 0.0)
    loss[0, 0] = jnp.sum(value)
    fits[0, 0] = jnp.sum(good).astype(jnp.int32)


def hidden_grad(scal, a0, b0, total, backs, head_t):
    width, depth = head_t.shape
    full = padded(width)
    a3, b1 = hop(a0, 1), hop(b0, -1)
    b3, a1 = hop(b0, 1), hop(a0, -1)
    a2, b2 = hop(a3, 1), hop(b1, -1)
    outs = (struct((ROWS // 2, depth), F32),) * 2 + (
        struct((1, 1), F32),
        struct((1, 1), jnp.int32),
    )
    return call(
        functools.partial(back_kernel, width),
        outs, scal, a0, b0, a1, b1, a2, b2, a3, b3, total, *backs, head_t,
        scratch=[pltpu.VMEM((LIVE, full), BF16), pltpu.VMEM((2 * ROWS, depth), BF16)],
        scalars=2,
    )


def pair_kernel(scal, mine, theirs, out, tiles):
    x = mine[...] + theirs[...]
    rows, half = x.shape[0], x.shape[1] // 2
    count = half // 128
    for k in (0, 1):
        for j in range(count):
            at = k * half + j * 128
            tiles[j, pl.ds(k, rows, 2), :] = x[:, at : at + 128]
    top = jnp.abs(tiles[0])
    for j in range(1, count):
        top = jnp.maximum(top, jnp.abs(tiles[j]))
    top = jnp.maximum(jnp.max(top, axis=1, keepdims=True), 1e-30)
    power = jnp.ceil(jnp.log2(top) + 0.001)
    scale = jnp.exp2(15.0 - power)
    for j in range(count):
        codes = (tiles[j] * scale + ROUND) - ROUND
        codes = jnp.minimum(codes, 32767.0).astype(jnp.int32)
        out[:, j * 128 : (j + 1) * 128] = codes.astype(I16)
    out[:, half:] = jnp.broadcast_to(power, (2 * rows, 128)).astype(jnp.int32).astype(I16)


def final_kernel(scal, got, out, square):
    half = got.shape[2] - 128
    total = jnp.zeros((8, half), F32)
    for chip in range(got.shape[0]):
        power = got[chip, :, half : half + 128].astype(jnp.int32).astype(F32)[:, 0:1]
        total += got[chip, :, :half].astype(jnp.int32).astype(F32) * jnp.exp2(power - 15.0)
    for row in range(4):
        for k in (0, 1):
            square[row : row + 1, k * half : (k + 1) * half] = total[2 * row + k : 2 * row + k + 1]
    out[...] = square[...].astype(BF16)


def pack_kernel(ids, valid, teacher, student, out):
    dt, ds = teacher.shape[1] // 2, student.shape[1] // 2
    line = iota((8, dt), 0)
    t = jnp.zeros((8, dt), F32)
    for row in range(4):
        for k in (0, 1):
            t = jnp.where(line == 2 * row + k, teacher[row : row + 1, k * dt : (k + 1) * dt].astype(F32), t)
    out[:, :, :dt] = jnp.broadcast_to(t.astype(BF16)[None], (32, 8, dt))
    line = iota((8, ds), 0)
    s = jnp.zeros((8, ds), F32)
    for row in range(4):
        for k in (0, 1):
            s = jnp.where(line == 2 * row + k, student[row : row + 1, k * ds : (k + 1) * ds].astype(F32), s)
    out[:, :, dt + 128 :] = jnp.broadcast_to(s.astype(BF16)[None], (32, 8, ds))
    line, lane = iota((8, 128), 0), iota((8, 128), 1)
    labels = jnp.zeros((8, 128), jnp.int32)
    for row in range(4):
        token = ids[row]
        for k, value in enumerate((token & 255, (token >> 8) & 255, token >> 16, valid[row])):
            labels = jnp.where((line == 2 * row) & (lane == k), value, labels)
    out[:, :, dt : dt + 128] = jnp.broadcast_to(labels.astype(F32).astype(BF16)[None], (32, 8, 128))


def hop(x, by):
    pairs = [(i, (i + by) % 4) for i in range(4)] + [(i + 4, (i - by) % 4 + 4) for i in range(4)]
    return lax.ppermute(x, ("c", "t"), pairs)


def swap_cores(x):
    return lax.ppermute(x, "c", [(0, 1), (1, 0)])


def spread(x, axes, n):
    return lax.all_to_all(
        jnp.broadcast_to(x[None], (n,) + x.shape), axes, split_axis=0, concat_axis=0, tiled=True
    )


def short_way(teacher_hidden, student_hidden, teacher_head, student_head, token_ids, valid):
    dt, ds = teacher_hidden.shape[1], student_hidden.shape[1]
    width = teacher_head.shape[1]
    full = padded(width)
    scal = jnp.stack(
        [lax.axis_index("t"), lax.axis_index("c"), lax.axis_index(VOCAB) * width]
    ).astype(jnp.int32)
    packed = pl.pallas_call(
        pack_kernel,
        out_shape=struct((32, 8, dt // 2 + 128 + ds // 2), BF16),
        in_specs=[SMEM, SMEM, VMEM, VMEM],
        out_specs=VMEM,
        compiler_params=pltpu.CompilerParams(vmem_limit_bytes=8 << 20),
    )(token_ids, valid, teacher_hidden, student_hidden)
    t_head, s_head = teacher_head.T, student_head.T
    own = lax.all_to_all(packed, CHIPS, split_axis=0, concat_axis=0, tiled=True)
    own = own.reshape(ROWS, packed.shape[2])
    other = swap_cores(own)
    one = (
        struct((GROUP, full), I16),
        struct((GROUP, full), I16),
        struct((GROUP, full), F32),
        struct((GROUP, full), F32),
        struct((8, 128), F32),
    )
    back_own, back_other, sampled, total, *made = call(
        functools.partial(front_kernel, width, ((0, 3, 1), (dt // 2 + 128, 1, 3))),
        (struct((ROWS // 2, 2 * ROWS), BF16),) * 2
        + (struct((GROUP, 128), F32), struct((8, 128), F32))
        + one + one,
        scal, own, other, t_head, s_head,
        scratch=[
            pltpu.VMEM((2, LIVE, ROWS), BF16),
            pltpu.VMEM((2, LIVE, ROWS), BF16),
            pltpu.VMEM((LIVE, dt), BF16),
            pltpu.VMEM((LIVE, ds), BF16),
            pltpu.VMEM(t_head.shape, BF16),
            pltpu.VMEM(s_head.shape, BF16),
            pltpu.VMEM((LIVE, full), F32),
            pltpu.SemaphoreType.DMA((2,)),
        ],
        streamed=2,
    )
    sums, peaks = [], []
    for (first, direct, mine, held, peak), by in ((made[:5], 1), (made[5:], -1)):
        late, late_peak = call(
            relay_kernel,
            (struct((GROUP, full), I16), struct((8, 128), F32)),
            scal, hop(first, by), held,
        )
        sums += [mine, hop(direct, -by), hop(late, by)]
        peaks += [peak, late_peak]
    t_logits, s_logits, stats = call(
        functools.partial(stats_kernel, width),
        (struct((GROUP, full), F32),) * 2 + (struct((8, 128), F32),),
        scal, *sums, sampled, *peaks,
        scratch=[pltpu.VMEM((128, 128), F32)],
    )
    (stats,) = call(merge_kernel, (struct((32, 8, 128), F32),), scal, stats, swap_cores(stats))
    every = lax.all_to_all(stats, CHIPS, split_axis=0, concat_axis=0, tiled=True)
    a0, b0 = call(
        functools.partial(grad_kernel, width),
        (struct((GROUP, LEFT), BF16), struct((GROUP, full - LEFT), BF16)),
        scal, every, t_logits, s_logits, sampled, total,
    )
    mine, theirs, loss, fits = hidden_grad(
        scal, a0, b0, total, (back_own, back_other), s_head
    )
    (pair,) = call(
        pair_kernel, (struct((ROWS, ds // 2 + 128), I16),), scal, mine, swap_cores(theirs),
        scratch=[pltpu.VMEM((ds // 256, ROWS, 128), F32)],
    )
    pair = pair.reshape(32, 8, ds // 2 + 128)
    got = lax.all_to_all(pair, CHIPS, split_axis=0, concat_axis=0, tiled=True)
    (grad,) = call(
        final_kernel, (struct((4, ds), BF16),), scal, got, scratch=[pltpu.VMEM((4, ds), F32)]
    )
    return loss.reshape(()), grad, fits.reshape(()) > 0


def long_way(teacher_hidden, student_hidden, teacher_head, student_head, token_ids, valid):
    ds = student_hidden.shape[1]
    width = teacher_head.shape[1]
    group = ROWS // 4
    labels = jnp.pad(jnp.stack([token_ids, valid]), ((0, 6), (0, 124)))
    labels = spread(labels, VOCAB, 64)[:, :2, :4].transpose(1, 0, 2).reshape(2, ROWS)

    def logits(hidden, head):
        rows = spread(hidden, VOCAB, 64).reshape(ROWS, hidden.shape[1])
        part = jnp.dot(rows, head, preferred_element_type=F32).reshape(4, group, width)
        return jnp.sum(lax.all_to_all(part, "t", split_axis=0, concat_axis=0, tiled=True), axis=0)

    teacher_logits = logits(teacher_hidden, teacher_head)
    student_logits = logits(student_hidden, student_head)
    here = lax.dynamic_slice_in_dim(labels, lax.axis_index("t") * group, group, 1)
    sampled, mask = here[0], here[1].astype(F32)
    columns = lax.axis_index(VOCAB) * width + jnp.arange(width, dtype=jnp.int32)
    onehot = columns[None, :] == sampled[:, None]
    t_top = jnp.max(teacher_logits, axis=1)
    s_top = jnp.max(student_logits, axis=1)
    t_exp = jnp.exp(teacher_logits - t_top[:, None])
    s_exp = jnp.exp(student_logits - s_top[:, None])
    stats = jnp.stack(
        [
            t_top,
            s_top,
            jnp.sum(t_exp, axis=1),
            jnp.sum(s_exp, axis=1),
            jnp.sum(t_exp * (teacher_logits - student_logits), axis=1),
            jnp.sum(jnp.where(onehot, student_logits, F32(0.0)), axis=1),
        ]
    )
    every = spread(jnp.pad(stats, ((0, 2), (0, 128 - group))), VOCAB, 64)[:, :, :group]
    teacher_top = jnp.max(every[:, 0], axis=0)
    student_top = jnp.max(every[:, 1], axis=0)
    t_scale = jnp.exp(every[:, 0] - teacher_top)
    s_scale = jnp.exp(every[:, 1] - student_top)
    teacher_total = jnp.sum(every[:, 2] * t_scale, axis=0)
    student_total = jnp.sum(every[:, 3] * s_scale, axis=0)
    cross_term = jnp.sum(every[:, 4] * t_scale, axis=0)
    picked = jnp.sum(every[:, 5], axis=0)
    teacher_lse = teacher_top + jnp.log(teacher_total)
    student_lse = student_top + jnp.log(student_total)
    per_row = cross_term / teacher_total - teacher_lse + 2.0 * student_lse - picked
    parts = spread(jnp.full((8, 128), jnp.sum(mask * per_row)), "t", 4)[:, 0, 0]
    loss = jnp.sum(parts) / jnp.sum(labels[1]).astype(F32)
    teacher_prob = jnp.exp(teacher_logits - teacher_lse[:, None])
    student_prob = jnp.exp(student_logits - student_lse[:, None])
    logit_grad = (
        mask[:, None] * (2.0 * student_prob - teacher_prob - onehot.astype(F32))
    ).astype(BF16)
    part = lax.dot_general(
        spread(logit_grad, "t", 4).reshape(ROWS, width), student_head, NT,
        preferred_element_type=F32,
    )
    got = lax.all_to_all(part.reshape(64, 4, ds), VOCAB, split_axis=0, concat_axis=0, tiled=True)
    return loss, jnp.sum(got, axis=0).astype(BF16)


def on_device(*args):
    loss, grad, fits = short_way(*args)
    return lax.cond(fits, lambda *_: (loss, grad), long_way, *args)


def solution(mesh):
    fine = Mesh(mesh.devices.reshape(4, 4, 2, 2, 4), VOCAB + ("t",))
    in_specs = (
        P(VOCAB, "t"),
        P(VOCAB, "t"),
        P("t", VOCAB),
        P("t", VOCAB),
        P(VOCAB),
        P(VOCAB),
    )
    return jax.shard_map(
        on_device, mesh=fine, in_specs=in_specs, out_specs=(P(), P(VOCAB, "t")), check_vma=False
    )
```

```python
import functools

import jax
import jax.numpy as jnp
from jax import lax
from jax.experimental import pallas as pl
from jax.experimental.pallas import tpu as pltpu
from jax.sharding import Mesh, PartitionSpec as P

VOCAB = ("y", "x", "zl", "c")
CHIPS = ("y", "x", "zl")
ROWS = 256
LIVE = 192
GROUP = LIVE // 4
LEFT = 1280
STEP = 1024.0
BOUND = 31.9
ROUND = 1.5 * 2.0**23
F32 = jnp.float32
BF16 = jnp.bfloat16
I16 = jnp.int16
NT = (((1,), (1,)), ((), ()))
VMEM = pl.BlockSpec(memory_space=pltpu.VMEM)
SMEM = pl.BlockSpec(memory_space=pltpu.SMEM)
ANY = pl.BlockSpec(memory_space=pl.ANY)


def struct(shape, dtype):
    return jax.ShapeDtypeStruct(shape, dtype)


def call(body, outs, *args, scratch=(), scalars=0, streamed=0):
    return pl.pallas_call(
        body,
        out_shape=outs,
        in_specs=[SMEM] + [VMEM] * (len(args) - 1 - streamed) + [ANY] * streamed,
        out_specs=[VMEM] * (len(outs) - scalars) + [SMEM] * scalars,
        scratch_shapes=scratch,
        compiler_params=pltpu.CompilerParams(vmem_limit_bytes=32 << 20),
    )(*args)


def padded(width):
    return -(-width // 128) * 128


def coded(x):
    return ((x * STEP + ROUND) - ROUND).astype(jnp.int32).astype(I16)


def decoded(x):
    return x.astype(jnp.int32).astype(F32) * (1.0 / STEP)


def iota(shape, axis):
    return lax.broadcasted_iota(jnp.int32, shape, axis)


def order(scal, own, other, at, pick_own, pick_other, back_own, back_other, sampled, total):
    me, core = scal[0], scal[1].astype(F32)
    wide = own.shape[0]
    line, lane = iota((wide, wide), 0), iota((wide, wide), 1)
    even = lane - lane % 2
    before = (line < even).astype(F32).astype(BF16)
    same = (line == even).astype(F32).astype(BF16)
    evens = (iota((wide, wide // 2), 0) == 2 * iota((wide, wide // 2), 1)).astype(F32).astype(BF16)
    found = []
    for ref in (own, other):
        labels = ref[:, at : at + 128].astype(F32).T[:8].astype(BF16)
        earlier = jnp.dot(labels, before, preferred_element_type=F32)[3:4]
        here = jnp.dot(labels, same, preferred_element_type=F32)
        ids = here[0:1] + 256.0 * here[1:2] + 65536.0 * here[2:3]
        found.append((here[3:4] > 0.5, earlier, ids, 0.5 * jnp.sum(here[3:4], keepdims=True)))
    start = (core * found[1][3], (1.0 - core) * found[0][3])
    picked = jnp.zeros((GROUP, 1), F32)
    for (ok, earlier, ids, _), base, pick, back in zip(
        found, start, (pick_own, pick_other), (back_own, back_other)
    ):
        slot = base + earlier
        group = jnp.floor(slot * (1.0 / GROUP) + 1e-3)
        turn = (group - me.astype(F32)) * (1.0 - 2.0 * core)
        turn = jnp.where(turn < 0.0, turn + 4.0, turn)
        near = slot + GROUP * (turn - group)
        near = jnp.where(ok & (slot < LIVE), near, -1.0)
        column = jnp.dot(
            jnp.broadcast_to(near, (8, wide)).astype(BF16), evens, preferred_element_type=F32
        ).T[:, 0:1]
        row = iota((LIVE, wide), 0).astype(F32)
        odd = iota((LIVE, wide), 1) % 2
        hit = row == near
        slots = (iota((wide // 2, 2 * ROWS), 1) % ROWS).astype(F32)
        back[...] = (slots == column).astype(F32).astype(BF16)
        for half in (0, 1):
            pick[half] = (hit & (odd == half)).astype(F32).astype(BF16)
        chosen = (hit & (odd == 0))[:GROUP]
        picked += jnp.sum(jnp.where(chosen, ids, 0.0), axis=1, keepdims=True)
    sampled[...] = jnp.broadcast_to(picked, sampled.shape)
    total[...] = jnp.broadcast_to(found[0][3] + found[1][3], total.shape)


def front_kernel(
    width, places, scal, own, other, t_head, s_head,
    back_own, back_other, sampled, total,
    t_first, t_direct, t_mine, t_held, t_peak, s_first, s_direct, s_mine, s_held, s_peak,
    pick_own, pick_other, t_rows, s_rows, t_loaded, s_loaded, logits, sems,
):
    full = padded(width)
    edge = full - 128
    g = GROUP
    copies = [
        pltpu.make_async_copy(head, loaded, sems.at[k])
        for k, (head, loaded) in enumerate(((t_head, t_loaded), (s_head, s_loaded)))
    ]
    for copy in copies:
        copy.start()
    order(
        scal, own, other, t_rows.shape[1] // 2,
        pick_own, pick_other, back_own, back_other, sampled, total,
    )
    logits[:, edge:full] = jnp.zeros((LIVE, 128), F32)
    for (at, near, relayed), copy, rows, loaded, (first, direct, mine, held, peak) in zip(
        places,
        copies,
        (t_rows, s_rows),
        (t_loaded, s_loaded),
        ((t_first, t_direct, t_mine, t_held, t_peak), (s_first, s_direct, s_mine, s_held, s_peak)),
    ):
        half = rows.shape[1] // 2
        for k in (0, 1):
            rows[:, k * half : (k + 1) * half] = (
                jnp.dot(pick_own[k], own[:, at : at + half], preferred_element_type=F32)
                + jnp.dot(pick_other[k], other[:, at : at + half], preferred_element_type=F32)
            ).astype(BF16)
        copy.wait()
        logits[:, :width] = lax.dot_general(
            rows[...], loaded[...], NT, preferred_element_type=F32
        )
        first[...] = coded(logits[2 * g : 3 * g])
        direct[...] = coded(logits[near * g : (near + 1) * g])
        mine[...] = logits[:g]
        held[...] = logits[relayed * g : (relayed + 1) * g]
        peak[...] = jnp.broadcast_to(jnp.max(jnp.abs(logits[g:]), keepdims=True), peak.shape)


def relay_kernel(scal, got, held, out, peak):
    total = held[...] + decoded(got[...])
    out[...] = coded(total)
    peak[...] = jnp.broadcast_to(jnp.max(jnp.abs(total), keepdims=True), peak.shape)


def stats_kernel(
    width, scal, t_mine, t_direct, t_late, s_mine, s_direct, s_late, sampled, p0, p1, p2, p3,
    t_out, s_out, stats, square,
):
    t = t_mine[...] + decoded(t_direct[...]) + decoded(t_late[...])
    s = s_mine[...] + decoded(s_direct[...]) + decoded(s_late[...])
    t_out[...] = t
    s_out[...] = s
    column = iota(t.shape, 1)
    inside = column < width
    onehot = (column + scal[2] == sampled[:, 0:1].astype(jnp.int32)) & inside
    t_top = jnp.max(jnp.where(inside, t, -jnp.inf), axis=1, keepdims=True)
    s_top = jnp.max(jnp.where(inside, s, -jnp.inf), axis=1, keepdims=True)
    t_exp = jnp.where(inside, jnp.exp(t - t_top), 0.0)
    s_exp = jnp.where(inside, jnp.exp(s - s_top), 0.0)
    values = (
        t_top,
        s_top,
        jnp.sum(t_exp, axis=1, keepdims=True),
        jnp.sum(s_exp, axis=1, keepdims=True),
        jnp.sum(t_exp * (t - s), axis=1, keepdims=True),
        jnp.sum(jnp.where(onehot, s, 0.0), axis=1, keepdims=True),
    )
    lane = iota((GROUP, 128), 1)
    board = jnp.zeros((GROUP, 128), F32)
    for k, value in enumerate(values):
        board = jnp.where(lane == k, value, board)
    square[...] = jnp.zeros(square.shape, F32)
    square[:GROUP] = board
    flipped = square[...].T[:8]
    peak = jnp.maximum(jnp.maximum(p0[...], p1[...]), jnp.maximum(p2[...], p3[...]))
    stats[...] = jnp.where(iota((8, 128), 0) == 6, peak, flipped)


def merge_kernel(scal, mine, theirs, out):
    a, b = mine[...], theirs[...]
    top = jnp.maximum(a, b)
    line = iota(a.shape, 0)
    scaled = []
    for x in (a, b):
        scale = jnp.exp(x - top)
        factor = jnp.where(line == 3, scale[1:2], jnp.where(line == 5, 1.0, scale[0:1]))
        scaled.append(x * factor)
    both = jnp.where((line < 2) | (line == 6), top, scaled[0] + scaled[1])
    out[...] = jnp.broadcast_to(both[None], out.shape)


def grad_kernel(width, scal, every, t_ref, s_ref, sampled, total, left, right):
    e = every[...]
    most = jnp.max(e, axis=0)
    t_top, s_top, peak = most[0:1], most[1:2], most[6:7]
    t_scale = jnp.exp(e[:, 0:1] - t_top[None])
    s_scale = jnp.exp(e[:, 1:2] - s_top[None])
    t_total = jnp.sum(e[:, 2:3] * t_scale, axis=0)
    s_total = jnp.sum(e[:, 3:4] * s_scale, axis=0)
    cross = jnp.sum(e[:, 4:5] * t_scale, axis=0)
    picked = jnp.sum(e[:, 5:6], axis=0)
    t_lse = t_top + jnp.log(t_total)
    s_lse = s_top + jnp.log(s_total)
    per_row = cross / t_total - t_lse + 2.0 * s_lse - picked
    first = scal[0] * GROUP
    count = total[0:1, 0:1].astype(jnp.int32)
    lane = iota((1, 128), 1)
    live = (lane < GROUP) & (lane + first < count)
    part = jnp.sum(jnp.where(live, per_row, 0.0), axis=1, keepdims=True)
    line = iota((8, 128), 0)
    turned = jnp.where(line == 0, t_lse, s_lse).T
    t_col, s_col = turned[:GROUP, 0:1], turned[:GROUP, 1:2]
    t, s = t_ref[...], s_ref[...]
    column = iota(t.shape, 1)
    onehot = (column + scal[2] == sampled[:, 0:1].astype(jnp.int32)).astype(F32)
    grad = 2.0 * jnp.exp(s - s_col) - jnp.exp(t - t_col) - onehot
    keep = (column < width) & (iota(t.shape, 0) + first < count)
    grad = jnp.where(keep, grad, 0.0)
    left[...] = grad[:, :LEFT].astype(BF16)
    right[...] = grad[:, LEFT:].astype(BF16)
    block = width // 128 * 128
    line, lane = iota((16, 128), 0), iota((16, 128), 1) + block - width
    tail = grad[:16, block : block + 128]
    for k, value in enumerate((part, jnp.max(peak, keepdims=True))):
        for piece in range(3):
            rounded = value.astype(BF16).astype(F32)
            tail = jnp.where((line == 0) & (lane == 3 * k + piece), rounded, tail)
            value = value - rounded
    right[:16, block - LEFT : block - LEFT + 128] = tail.astype(BF16)


def back_kernel(
    width, scal, a0, b0, a1, b1, a2, b2, a3, b3, total, back_other, head,
    theirs, parts, loss, fits, grads,
):
    for k, (a, b) in enumerate(((a0, b0), (a1, b1), (a2, b2), (a3, b3))):
        grads[k * GROUP : (k + 1) * GROUP, :LEFT] = a[...]
        grads[k * GROUP : (k + 1) * GROUP, LEFT:] = b[...]
    x = jnp.dot(grads[:, :width], head[...], preferred_element_type=F32)
    high = x.astype(BF16)
    low = (x - high.astype(F32)).astype(BF16)
    for k, part in enumerate((high, low)):
        parts[k * ROWS : k * ROWS + LIVE] = part
        parts[k * ROWS + LIVE : (k + 1) * ROWS] = jnp.zeros((ROWS - LIVE, x.shape[1]), BF16)
    theirs[...] = jnp.dot(back_other[...], parts[...], preferred_element_type=F32)
    block = width // 128 * 128
    line, lane = iota((16, 128), 0), iota((16, 128), 1) + block - width
    block -= LEFT
    sums, peaks = [], []
    for ref in (b0, b1, b2, b3):
        tail = jnp.where(line == 0, ref[:16, block : block + 128].astype(F32), 0.0)
        sums.append(jnp.sum(jnp.where((lane >= 0) & (lane < 3), tail, 0.0), keepdims=True))
        peaks.append(jnp.sum(jnp.where((lane >= 3) & (lane < 6), tail, 0.0), keepdims=True))
    count = total[0:1, 0:1]
    value = ((sums[0] + sums[2]) + (sums[1] + sums[3])) / count
    peak = jnp.maximum(jnp.maximum(peaks[0], peaks[1]), jnp.maximum(peaks[2], peaks[3]))
    good = jnp.where((count <= LIVE) & (peak < BOUND), 1.0, 0.0)
    loss[0, 0] = jnp.sum(value)
    fits[0, 0] = jnp.sum(good).astype(jnp.int32)


def place_kernel(scal, back, parts, out):
    out[...] = jnp.dot(back[...], parts[...], preferred_element_type=F32)


def hidden_grad(scal, a0, b0, total, backs, head_t):
    width, depth = head_t.shape
    full = padded(width)
    a3, b1 = hop(a0, 1), hop(b0, -1)
    b3, a1 = hop(b0, 1), hop(a0, -1)
    a2, b2 = hop(a3, 1), hop(b1, -1)
    outs = (
        struct((ROWS // 2, depth), F32),
        struct((2 * ROWS, depth), BF16),
        struct((1, 1), F32),
        struct((1, 1), jnp.int32),
    )
    return call(
        functools.partial(back_kernel, width),
        outs, scal, a0, b0, a1, b1, a2, b2, a3, b3, total, backs[1], head_t,
        scratch=[pltpu.VMEM((LIVE, full), BF16)],
        scalars=2,
    )


def pair_kernel(scal, mine, theirs, out, tiles):
    x = mine[...] + theirs[...]
    rows, half = x.shape[0], x.shape[1] // 2
    count = half // 128
    for k in (0, 1):
        for j in range(count):
            at = k * half + j * 128
            tiles[j, pl.ds(k, rows, 2), :] = x[:, at : at + 128]
    top = jnp.abs(tiles[0])
    for j in range(1, count):
        top = jnp.maximum(top, jnp.abs(tiles[j]))
    top = jnp.maximum(jnp.max(top, axis=1, keepdims=True), 1e-30)
    power = jnp.ceil(jnp.log2(top) + 0.001)
    scale = jnp.exp2(15.0 - power)
    for j in range(count):
        codes = (tiles[j] * scale + ROUND) - ROUND
        codes = jnp.minimum(codes, 32767.0).astype(jnp.int32)
        out[:, j * 128 : (j + 1) * 128] = codes.astype(I16)
    out[:, half:] = jnp.broadcast_to(power, (2 * rows, 128)).astype(jnp.int32).astype(I16)


def final_kernel(scal, got, out, square):
    half = got.shape[2] - 128
    total = jnp.zeros((8, half), F32)
    for chip in range(got.shape[0]):
        power = got[chip, :, half : half + 128].astype(jnp.int32).astype(F32)[:, 0:1]
        total += got[chip, :, :half].astype(jnp.int32).astype(F32) * jnp.exp2(power - 15.0)
    for row in range(4):
        for k in (0, 1):
            square[row : row + 1, k * half : (k + 1) * half] = total[2 * row + k : 2 * row + k + 1]
    out[...] = square[...].astype(BF16)


def pack_kernel(ids, valid, teacher, student, out):
    dt, ds = teacher.shape[1] // 2, student.shape[1] // 2
    line = iota((8, dt), 0)
    t = jnp.zeros((8, dt), F32)
    for row in range(4):
        for k in (0, 1):
            t = jnp.where(line == 2 * row + k, teacher[row : row + 1, k * dt : (k + 1) * dt].astype(F32), t)
    out[:, :, :dt] = jnp.broadcast_to(t.astype(BF16)[None], (32, 8, dt))
    line = iota((8, ds), 0)
    s = jnp.zeros((8, ds), F32)
    for row in range(4):
        for k in (0, 1):
            s = jnp.where(line == 2 * row + k, student[row : row + 1, k * ds : (k + 1) * ds].astype(F32), s)
    out[:, :, dt + 128 :] = jnp.broadcast_to(s.astype(BF16)[None], (32, 8, ds))
    line, lane = iota((8, 128), 0), iota((8, 128), 1)
    labels = jnp.zeros((8, 128), jnp.int32)
    for row in range(4):
        token = ids[row]
        for k, value in enumerate((token & 255, (token >> 8) & 255, token >> 16, valid[row])):
            labels = jnp.where((line == 2 * row) & (lane == k), value, labels)
    out[:, :, dt : dt + 128] = jnp.broadcast_to(labels.astype(F32).astype(BF16)[None], (32, 8, 128))


def hop(x, by):
    pairs = [(i, (i + by) % 4) for i in range(4)] + [(i + 4, (i - by) % 4 + 4) for i in range(4)]
    return lax.ppermute(x, ("c", "t"), pairs)


def swap_cores(x):
    return lax.ppermute(x, "c", [(0, 1), (1, 0)])


def spread(x, axes, n):
    return lax.all_to_all(
        jnp.broadcast_to(x[None], (n,) + x.shape), axes, split_axis=0, concat_axis=0, tiled=True
    )


def short_way(teacher_hidden, student_hidden, teacher_head, student_head, token_ids, valid):
    dt, ds = teacher_hidden.shape[1], student_hidden.shape[1]
    width = teacher_head.shape[1]
    full = padded(width)
    scal = jnp.stack(
        [lax.axis_index("t"), lax.axis_index("c"), lax.axis_index(VOCAB) * width]
    ).astype(jnp.int32)
    packed = pl.pallas_call(
        pack_kernel,
        out_shape=struct((32, 8, dt // 2 + 128 + ds // 2), BF16),
        in_specs=[SMEM, SMEM, VMEM, VMEM],
        out_specs=VMEM,
        compiler_params=pltpu.CompilerParams(vmem_limit_bytes=8 << 20),
    )(token_ids, valid, teacher_hidden, student_hidden)
    t_head, s_head = teacher_head.T, student_head.T
    own = lax.all_to_all(packed, CHIPS, split_axis=0, concat_axis=0, tiled=True)
    own = own.reshape(ROWS, packed.shape[2])
    other = swap_cores(own)
    one = (
        struct((GROUP, full), I16),
        struct((GROUP, full), I16),
        struct((GROUP, full), F32),
        struct((GROUP, full), F32),
        struct((8, 128), F32),
    )
    back_own, back_other, sampled, total, *made = call(
        functools.partial(front_kernel, width, ((0, 3, 1), (dt // 2 + 128, 1, 3))),
        (struct((ROWS // 2, 2 * ROWS), BF16),) * 2
        + (struct((GROUP, 128), F32), struct((8, 128), F32))
        + one + one,
        scal, own, other, t_head, s_head,
        scratch=[
            pltpu.VMEM((2, LIVE, ROWS), BF16),
            pltpu.VMEM((2, LIVE, ROWS), BF16),
            pltpu.VMEM((LIVE, dt), BF16),
            pltpu.VMEM((LIVE, ds), BF16),
            pltpu.VMEM(t_head.shape, BF16),
            pltpu.VMEM(s_head.shape, BF16),
            pltpu.VMEM((LIVE, full), F32),
            pltpu.SemaphoreType.DMA((2,)),
        ],
        streamed=2,
    )
    sums, peaks = [], []
    for (first, direct, mine, held, peak), by in ((made[:5], 1), (made[5:], -1)):
        late, late_peak = call(
            relay_kernel,
            (struct((GROUP, full), I16), struct((8, 128), F32)),
            scal, hop(first, by), held,
        )
        sums += [mine, hop(direct, -by), hop(late, by)]
        peaks += [peak, late_peak]
    t_logits, s_logits, stats = call(
        functools.partial(stats_kernel, width),
        (struct((GROUP, full), F32),) * 2 + (struct((8, 128), F32),),
        scal, *sums, sampled, *peaks,
        scratch=[pltpu.VMEM((128, 128), F32)],
    )
    (stats,) = call(merge_kernel, (struct((32, 8, 128), F32),), scal, stats, swap_cores(stats))
    every = lax.all_to_all(stats, CHIPS, split_axis=0, concat_axis=0, tiled=True)
    a0, b0 = call(
        functools.partial(grad_kernel, width),
        (struct((GROUP, LEFT), BF16), struct((GROUP, full - LEFT), BF16)),
        scal, every, t_logits, s_logits, sampled, total,
    )
    theirs, parts, loss, fits = hidden_grad(
        scal, a0, b0, total, (back_own, back_other), s_head
    )
    (mine,) = call(place_kernel, (struct(theirs.shape, F32),), scal, back_own, parts)
    (pair,) = call(
        pair_kernel, (struct((ROWS, ds // 2 + 128), I16),), scal, mine, swap_cores(theirs),
        scratch=[pltpu.VMEM((ds // 256, ROWS, 128), F32)],
    )
    pair = pair.reshape(32, 8, ds // 2 + 128)
    got = lax.all_to_all(pair, CHIPS, split_axis=0, concat_axis=0, tiled=True)
    (grad,) = call(
        final_kernel, (struct((4, ds), BF16),), scal, got, scratch=[pltpu.VMEM((4, ds), F32)]
    )
    return loss.reshape(()), grad, fits.reshape(()) > 0


def long_way(teacher_hidden, student_hidden, teacher_head, student_head, token_ids, valid):
    ds = student_hidden.shape[1]
    width = teacher_head.shape[1]
    group = ROWS // 4
    labels = jnp.pad(jnp.stack([token_ids, valid]), ((0, 6), (0, 124)))
    labels = spread(labels, VOCAB, 64)[:, :2, :4].transpose(1, 0, 2).reshape(2, ROWS)

    def logits(hidden, head):
        rows = spread(hidden, VOCAB, 64).reshape(ROWS, hidden.shape[1])
        part = jnp.dot(rows, head, preferred_element_type=F32).reshape(4, group, width)
        return jnp.sum(lax.all_to_all(part, "t", split_axis=0, concat_axis=0, tiled=True), axis=0)

    teacher_logits = logits(teacher_hidden, teacher_head)
    student_logits = logits(student_hidden, student_head)
    here = lax.dynamic_slice_in_dim(labels, lax.axis_index("t") * group, group, 1)
    sampled, mask = here[0], here[1].astype(F32)
    columns = lax.axis_index(VOCAB) * width + jnp.arange(width, dtype=jnp.int32)
    onehot = columns[None, :] == sampled[:, None]
    t_top = jnp.max(teacher_logits, axis=1)
    s_top = jnp.max(student_logits, axis=1)
    t_exp = jnp.exp(teacher_logits - t_top[:, None])
    s_exp = jnp.exp(student_logits - s_top[:, None])
    stats = jnp.stack(
        [
            t_top,
            s_top,
            jnp.sum(t_exp, axis=1),
            jnp.sum(s_exp, axis=1),
            jnp.sum(t_exp * (teacher_logits - student_logits), axis=1),
            jnp.sum(jnp.where(onehot, student_logits, F32(0.0)), axis=1),
        ]
    )
    every = spread(jnp.pad(stats, ((0, 2), (0, 128 - group))), VOCAB, 64)[:, :, :group]
    teacher_top = jnp.max(every[:, 0], axis=0)
    student_top = jnp.max(every[:, 1], axis=0)
    t_scale = jnp.exp(every[:, 0] - teacher_top)
    s_scale = jnp.exp(every[:, 1] - student_top)
    teacher_total = jnp.sum(every[:, 2] * t_scale, axis=0)
    student_total = jnp.sum(every[:, 3] * s_scale, axis=0)
    cross_term = jnp.sum(every[:, 4] * t_scale, axis=0)
    picked = jnp.sum(every[:, 5], axis=0)
    teacher_lse = teacher_top + jnp.log(teacher_total)
    student_lse = student_top + jnp.log(student_total)
    per_row = cross_term / teacher_total - teacher_lse + 2.0 * student_lse - picked
    parts = spread(jnp.full((8, 128), jnp.sum(mask * per_row)), "t", 4)[:, 0, 0]
    loss = jnp.sum(parts) / jnp.sum(labels[1]).astype(F32)
    teacher_prob = jnp.exp(teacher_logits - teacher_lse[:, None])
    student_prob = jnp.exp(student_logits - student_lse[:, None])
    logit_grad = (
        mask[:, None] * (2.0 * student_prob - teacher_prob - onehot.astype(F32))
    ).astype(BF16)
    part = lax.dot_general(
        spread(logit_grad, "t", 4).reshape(ROWS, width), student_head, NT,
        preferred_element_type=F32,
    )
    got = lax.all_to_all(part.reshape(64, 4, ds), VOCAB, split_axis=0, concat_axis=0, tiled=True)
    return loss, jnp.sum(got, axis=0).astype(BF16)


def on_device(*args):
    loss, grad, fits = short_way(*args)
    return lax.cond(fits, lambda *_: (loss, grad), long_way, *args)


def solution(mesh):
    fine = Mesh(mesh.devices.reshape(4, 4, 2, 2, 4), VOCAB + ("t",))
    in_specs = (
        P(VOCAB, "t"),
        P(VOCAB, "t"),
        P("t", VOCAB),
        P("t", VOCAB),
        P(VOCAB),
        P(VOCAB),
    )
    return jax.shard_map(
        on_device, mesh=fine, in_specs=in_specs, out_specs=(P(), P(VOCAB, "t")), check_vma=False
    )
```
